32 devices in a mesh: seq: 8 (over z, x), tp: 4 (over y, core).
Axes of the slice: x: 2, y: 2, z: 4, core: 2. Of those that a mesh axis runs over, the one named last changes fastest.
Arguments:
- hidden: bfloat16 [2048, 8192], P('seq', 'tp'), may hold values from -6 to 6
- query_base: bfloat16 [2048, 4096], P('seq', 'tp'), may hold values from -150 to 150
- rotated_key_cache: bfloat16 [2048, 1024], P('seq', 'tp'), may hold values from -7 to 7
- frozen_value_base: bfloat16 [2048, 1024], P('seq', 'tp'), may hold values from -6 to 6
- output_cotangent: bfloat16 [2048, 4096], P('seq', 'tp'), may hold values from -0.9 to 0.9
- qdown_mean: float32 [16, 8192], P(None, 'tp'), may hold values from -0.0625 to 0.0625
- qdown_sigma: float32 [16, 8192], P(None, 'tp'), may hold values from 0.004 to 0.012
- qdown_noise: float32 [16, 8192], P(None, 'tp'), may hold values from -4 to 4
- qup_mean: float32 [16, 4096], P(None, 'tp'), may hold values from -1.5 to 1.5
- qup_sigma: float32 [16, 4096], P(None, 'tp'), may hold values from 0.08 to 0.25
- qup_noise: float32 [16, 4096], P(None, 'tp'), may hold values from -4 to 4
- vdown_mean: float32 [16, 8192], P(None, 'tp'), may hold values from -0.0625 to 0.0625
- vdown_sigma: float32 [16, 8192], P(None, 'tp'), may hold values from 0.004 to 0.012
- vdown_noise: float32 [16, 8192], P(None, 'tp'), may hold values from -4 to 4
- value_up_mean: float32 [16, 1024], P(None, 'tp'), may hold values from -1.5 to 1.5
- value_up_deviation: float32 [16, 1024], P(None, 'tp'), may hold values from 0.08 to 0.25
- value_up_noise: float32 [16, 1024], P(None, 'tp'), may hold values from -4 to 4
Outputs:
- qdown_gmean: float32 [16, 8192], P(None, 'tp')
- qdown_gsigma: float32 [16, 8192], P(None, 'tp')
- qup_gmean: float32 [16, 4096], P(None, 'tp')
- qup_gsigma: float32 [16, 4096], P(None, 'tp')
- vdown_gmean: float32 [16, 8192], P(None, 'tp')
- vdown_gsigma: float32 [16, 8192], P(None, 'tp')
- vup_gmean: float32 [16, 1024], P(None, 'tp')
- vup_gsigma: float32 [16, 1024], P(None, 'tp')
The draws below stay inside these ranges and needn't reach their ends.
All inputs are finite; a program needn't handle non-finite values.
Results may differ from the reference program's by a relative error of at most 0.0075.
The reference program's roundings to bfloat16 on the way count: a program that leaves them out, or rounds other values in their place, can miss the bound.
Values may be sent and summed in bfloat16 or wider, within the bound.
A program may use at most 64 MiB of HBM per device.

```python
import math
import jax
import jax.numpy as jnp
from jax import lax

D = 8192
QUERY_HEADS = 32
KEY_VALUE_HEADS = 8
HEAD_SIZE = 128
ADAPTER_RANK = 16
SEQUENCE_LENGTH = 2048


def joint_draw(key):
    key_portion = jnp.clip(jax.random.normal(jax.random.fold_in(key, 7101), (SEQUENCE_LENGTH, KEY_VALUE_HEADS * HEAD_SIZE), jnp.float32), -6.0, 6.0)
    query_part = jnp.clip(jax.random.normal(jax.random.fold_in(key, 7102), (SEQUENCE_LENGTH, QUERY_HEADS * HEAD_SIZE), jnp.float32), -6.0, 6.0)
    return (query_part, key_portion)


def draw_query_base(key, part):
    return joint_draw(key)[0].astype(jnp.bfloat16)


def draw_rotated_key_cache(key, part):
    return joint_draw(key)[1].astype(jnp.bfloat16)


def draw_output_cotangent(key, part):
    along = jnp.arange(SEQUENCE_LENGTH, dtype=jnp.float32) / (SEQUENCE_LENGTH - 1.0)
    ramp = 1.0 + 2.0 * along
    values = jnp.clip(jax.random.normal(jax.random.fold_in(key, 7201), (SEQUENCE_LENGTH, QUERY_HEADS * HEAD_SIZE), jnp.float32), -6.0, 6.0)
    result = 0.05 * values * ramp[:, None]
    return result.astype(jnp.bfloat16)


def levels(own_key, dims, split, smallest, top_value):
    def one(dim, blocks):
        heights = jax.random.uniform(jax.random.fold_in(jax.random.fold_in(own_key, 6), dim), (blocks,), jnp.float32, smallest / len(split), top_value / len(split))
        return jnp.repeat(jnp.exp(heights), dims[dim] // blocks).reshape((-1,) + (1,) * (len(dims) - dim - 1))

    loudness = one(*split[0])
    for cut in split[1:]:
        loudness = loudness * one(*cut)
    return loudness


def gaussian(rng, extent, scale, reach, pieces=(), kind=jnp.bfloat16):
    values = jax.random.normal(rng, extent, jnp.float32) * scale
    if len(pieces) > 0:
        values = levels(rng, extent, pieces, -0.22, 0.18) * values
    return jnp.clip(values, min=-reach, max=reach).astype(kind)


def setup_inputs(seed: int = 0) -> dict:
    arg_keys = jax.random.split(jax.random.key(seed), 18)
    return {
        "hidden": gaussian(arg_keys[0], (SEQUENCE_LENGTH, D), 1.0, 6.0, ((0, 8), (1, 4))),
        "query_base": draw_query_base(jax.random.fold_in(arg_keys[17], 71), 0),
        "rotated_key_cache": draw_rotated_key_cache(jax.random.fold_in(arg_keys[17], 71), 0),
        "frozen_value_base": gaussian(arg_keys[3], (SEQUENCE_LENGTH, KEY_VALUE_HEADS * HEAD_SIZE), 1.0, 6.0, ((0, 8), (1, 4))),
        "output_cotangent": draw_output_cotangent(jax.random.fold_in(arg_keys[17], 71), 0),
        "qdown_mean": gaussian(arg_keys[5], (ADAPTER_RANK, D), D ** -0.5, 0.0625, ((1, 4),), jnp.float32),
        "qdown_sigma": jnp.clip(jnp.exp(math.log(0.012) - 1.09861225 * jax.random.uniform(arg_keys[6], (ADAPTER_RANK, D), jnp.float32) ** levels(arg_keys[6], (ADAPTER_RANK, D), ((1, 4),), -0.2, 0.2)), 0.004, 0.012),
        "qdown_noise": gaussian(arg_keys[7], (ADAPTER_RANK, D), 1.0, 4.0, ((1, 4),), jnp.float32),
        "qup_mean": gaussian(arg_keys[8], (ADAPTER_RANK, QUERY_HEADS * HEAD_SIZE), ADAPTER_RANK ** -0.5, 1.5, ((1, 4),), jnp.float32),
        "qup_sigma": jnp.clip(jnp.exp(math.log(0.25) - 1.1394343 * jax.random.uniform(arg_keys[9], (ADAPTER_RANK, QUERY_HEADS * HEAD_SIZE), jnp.float32) ** levels(arg_keys[9], (ADAPTER_RANK, QUERY_HEADS * HEAD_SIZE), ((1, 4),), -0.2, 0.2)), 0.08, 0.25),
        "qup_noise": gaussian(arg_keys[10], (ADAPTER_RANK, QUERY_HEADS * HEAD_SIZE), 1.0, 4.0, ((1, 4),), jnp.float32),
        "vdown_mean": gaussian(arg_keys[11], (ADAPTER_RANK, D), D ** -0.5, 0.0625, ((1, 4),), jnp.float32),
        "vdown_sigma": jnp.clip(jnp.exp(math.log(0.012) - 1.09861225 * jax.random.uniform(arg_keys[12], (ADAPTER_RANK, D), jnp.float32) ** levels(arg_keys[12], (ADAPTER_RANK, D), ((1, 4),), -0.2, 0.2)), 0.004, 0.012),
        "vdown_noise": gaussian(arg_keys[13], (ADAPTER_RANK, D), 1.0, 4.0, ((1, 4),), jnp.float32),
        "value_up_mean": gaussian(arg_keys[14], (ADAPTER_RANK, KEY_VALUE_HEADS * HEAD_SIZE), ADAPTER_RANK ** -0.5, 1.5, ((1, 4),), jnp.float32),
        "value_up_deviation": jnp.clip(jnp.exp(math.log(0.25) - 1.1394343 * jax.random.uniform(arg_keys[15], (ADAPTER_RANK, KEY_VALUE_HEADS * HEAD_SIZE), jnp.float32) ** levels(arg_keys[15], (ADAPTER_RANK, KEY_VALUE_HEADS * HEAD_SIZE), ((1, 4),), -0.2, 0.2)), 0.08, 0.25),
        "value_up_noise": gaussian(arg_keys[16], (ADAPTER_RANK, KEY_VALUE_HEADS * HEAD_SIZE), 1.0, 4.0, ((1, 4),), jnp.float32),
    }


def sample(mean, sigma, noise):
    return (mean + sigma * noise).astype(jnp.bfloat16)


def head_grads(query_g, key_g, value_g, grad_g):
    query_group = QUERY_HEADS // KEY_VALUE_HEADS
    scale = HEAD_SIZE ** -0.5
    qblock = math.gcd(SEQUENCE_LENGTH, 512)
    blocks = SEQUENCE_LENGTH // qblock
    key_pos = jnp.arange(SEQUENCE_LENGTH, dtype=jnp.int32)

    def advance(dv_acc, index):
        start = (index * qblock).astype(jnp.int32)
        rows_q = lax.dynamic_slice_in_dim(query_g, start, qblock, 0).reshape(qblock * query_group, HEAD_SIZE)
        rows_d = lax.dynamic_slice_in_dim(grad_g, start, qblock, 0).reshape(qblock * query_group, HEAD_SIZE)
        row_pos = start + jnp.arange(qblock * query_group, dtype=jnp.int32) // query_group
        mask = key_pos[None, :] <= row_pos[:, None]
        scores = jnp.dot(rows_q, key_g.T, preferred_element_type=jnp.float32) * scale
        masked = jnp.where(mask, scores, -jnp.inf)
        top = jnp.max(masked, axis=1, keepdims=True)
        total = jnp.sum(jnp.exp(masked - top), axis=1, keepdims=True)
        lse = top + jnp.log(total)
        probs = jnp.exp(masked - lse)
        dprob = jnp.dot(rows_d, value_g.T, preferred_element_type=jnp.float32)
        delta = jnp.sum(probs * dprob, axis=1, keepdims=True)
        dscore = (probs * (dprob - delta)).astype(jnp.bfloat16)
        dquery = (jnp.dot(dscore, key_g, preferred_element_type=jnp.float32) * scale).astype(jnp.bfloat16)
        dv_acc = dv_acc + jnp.dot(probs.astype(jnp.bfloat16).T, rows_d, preferred_element_type=jnp.float32)
        return dv_acc, dquery.reshape(qblock, query_group * HEAD_SIZE)

    dv_acc, dq_blocks = lax.scan(advance, jnp.zeros((SEQUENCE_LENGTH, HEAD_SIZE), jnp.float32), jnp.arange(blocks, dtype=jnp.int32))
    return dq_blocks.reshape(SEQUENCE_LENGTH, query_group * HEAD_SIZE), dv_acc.astype(jnp.bfloat16)


def reference(hidden, query_base, rotated_key_cache, frozen_value_base, output_cotangent, qdown_mean, qdown_sigma, qdown_noise, qup_mean, qup_sigma, qup_noise, vdown_mean, vdown_sigma, vdown_noise, value_up_mean, value_up_deviation, value_up_noise):
    query_group = QUERY_HEADS // KEY_VALUE_HEADS
    qdown = sample(qdown_mean, qdown_sigma, qdown_noise)
    qup = sample(qup_mean, qup_sigma, qup_noise)
    vdown = sample(vdown_mean, vdown_sigma, vdown_noise)
    vup = sample(value_up_mean, value_up_deviation, value_up_noise)
    qlow = jnp.dot(hidden, qdown.T, preferred_element_type=jnp.float32).astype(jnp.bfloat16)
    vlow = jnp.dot(hidden, vdown.T, preferred_element_type=jnp.float32).astype(jnp.bfloat16)
    query_input = (query_base.astype(jnp.float32) + jnp.dot(qlow, qup, preferred_element_type=jnp.float32)).astype(jnp.bfloat16)
    value_input = (frozen_value_base.astype(jnp.float32) + jnp.dot(vlow, vup, preferred_element_type=jnp.float32)).astype(jnp.bfloat16)
    head_queries = query_input.reshape(SEQUENCE_LENGTH, KEY_VALUE_HEADS, query_group * HEAD_SIZE).transpose(1, 0, 2)
    head_output_gradient = output_cotangent.reshape(SEQUENCE_LENGTH, KEY_VALUE_HEADS, query_group * HEAD_SIZE).transpose(1, 0, 2)
    head_keys = rotated_key_cache.reshape(SEQUENCE_LENGTH, KEY_VALUE_HEADS, HEAD_SIZE).transpose(1, 0, 2)
    head_values = value_input.reshape(SEQUENCE_LENGTH, KEY_VALUE_HEADS, HEAD_SIZE).transpose(1, 0, 2)
    dq_h, value_head_gradient = lax.map(lambda items: head_grads(items[0], items[1], items[2], items[3]), (head_queries, head_keys, head_values, head_output_gradient))
    dquery = dq_h.transpose(1, 0, 2).reshape(SEQUENCE_LENGTH, QUERY_HEADS * HEAD_SIZE)
    value_gradient = value_head_gradient.transpose(1, 0, 2).reshape(SEQUENCE_LENGTH, KEY_VALUE_HEADS * HEAD_SIZE)
    qup_grad = jnp.dot(qlow.T, dquery, preferred_element_type=jnp.float32)
    vup_grad = jnp.dot(vlow.T, value_gradient, preferred_element_type=jnp.float32)
    qlow_grad = jnp.dot(dquery, qup.T, preferred_element_type=jnp.float32).astype(jnp.bfloat16)
    vlow_grad = jnp.dot(value_gradient, vup.T, preferred_element_type=jnp.float32).astype(jnp.bfloat16)
    qdown_grad = jnp.dot(qlow_grad.T, hidden, preferred_element_type=jnp.float32)
    vdown_grad = jnp.dot(vlow_grad.T, hidden, preferred_element_type=jnp.float32)
    return (qdown_grad, qdown_grad * qdown_noise, qup_grad, qup_grad * qup_noise, vdown_grad, vdown_grad * vdown_noise, vup_grad, vup_grad * value_up_noise)
```

```python
import functools
import math

import jax
import jax.numpy as jnp
from jax import lax
from jax.experimental import pallas as pl
from jax.experimental.pallas import tpu as pltpu
from jax.sharding import PartitionSpec as P

HEAD = 128
RANK = 16
GROUP = 4
F32 = jnp.float32
BF16 = jnp.bfloat16
NEG = -1e30


def nt(a, b):
    return lax.dot_general(a, b, (((1,), (1,)), ((), ())), preferred_element_type=F32)


def tn(a, b):
    return lax.dot_general(a, b, (((0,), (0,)), ((), ())), preferred_element_type=F32)


def nn(a, b):
    return jnp.dot(a, b, preferred_element_type=F32)


def kernel(
    n, m, units, per,
    hidden, qbase, kc, vb, og,
    qdm, qds, qdn, qum, qus, qun, vdm, vds, vdn, vum, vus, vun,
    o_qd, o_qds, o_qu, o_qus, o_vd, o_vds, o_vu, o_vus,
    kall, vall, vlow_all, lowx, gx, qs, dos, top, tot, wei, dqt, vgs, vgx, vug, quw, pack, rsx, agx,
    k_s, k_r, v_s, v_r, l_s, l_r, x_s, x_r, y_s, y_r, g_s, g_r, r_s, r_r, a_s, a_r,
):
    T, DL = hidden.shape
    KV = kc.shape[1] // HEAD
    rows = GROUP * T
    scale = HEAD ** -0.5
    c2 = scale * math.log2(math.e)
    me = lax.axis_index("seq")
    t = lax.axis_index("tp")

    def to_seq(src, dst, ss, rs, who):
        return pltpu.make_async_remote_copy(
            src_ref=src, dst_ref=dst, send_sem=ss, recv_sem=rs,
            device_id=(who, t), device_id_type=pl.DeviceIdType.MESH,
        )

    def to_tp(src, dst, ss, rs, who):
        return pltpu.make_async_remote_copy(
            src_ref=src, dst_ref=dst, send_sem=ss, recv_sem=rs,
            device_id=(me, who), device_id_type=pl.DeviceIdType.MESH,
        )

    def loop(lo, hi, body):
        def step(i, c):
            body(i)
            return c
        lax.fori_loop(lo, hi, step, 0)

    barrier = pltpu.get_barrier_semaphore()

    def greet_seq(d):
        pl.semaphore_signal(
            barrier, inc=1, device_id=(lax.rem(me + d, n), t),
            device_id_type=pl.DeviceIdType.MESH,
        )

    def greet_tp(d):
        pl.semaphore_signal(
            barrier, inc=1, device_id=(me, lax.rem(t + d, m)),
            device_id_type=pl.DeviceIdType.MESH,
        )

    loop(1, n, greet_seq)
    loop(1, m, greet_tp)
    pl.semaphore_wait(barrier, n + m - 2)

    def k_copy(who):
        return to_seq(kc, kall.at[me], k_s.at[who], k_r.at[me], who)

    def v_copy(who):
        return to_seq(vb, vall.at[me], v_s.at[who], v_r.at[me], who)

    def send_kv(who):
        k_copy(who).start()
        v_copy(who).start()

    loop(me + 1, n, send_kv)

    qup = (qum[...] + qus[...] * qun[...]).astype(BF16)
    vup = (vum[...] + vus[...] * vun[...]).astype(BF16)
    qdown = (qdm[...] + qds[...] * qdn[...]).astype(BF16)
    vdown = (vdm[...] + vds[...] * vdn[...]).astype(BF16)
    lowx[t] = jnp.concatenate([nt(qdown, hidden[...]), nt(vdown, hidden[...])], axis=0)

    def x_copy(who):
        return to_tp(lowx.at[t], lowx.at[t], x_s.at[who], x_r.at[t], who)

    def x_in(who):
        return to_tp(lowx.at[who], lowx.at[who], x_s.at[who], x_r.at[who], who)

    loop(1, m, lambda d: x_copy(lax.rem(t + d, m)).start())
    for g in range(KV):
        for h in range(GROUP):
            at = (g * GROUP + h) * HEAD
            dos[g, h * T:(h + 1) * T, :] = og[:, at:at + HEAD]
    loop(1, m, lambda d: x_in(lax.rem(t + d, m)).wait_recv())
    low = lowx[0]
    for i in range(1, m):
        low = low + lowx[i]
    low = low.astype(BF16)
    qlow = low[:RANK]
    vlow = low[RANK:]
    vlow_all[me] = vlow

    def l_copy(who):
        return to_seq(vlow_all.at[me], vlow_all.at[me], l_s.at[who], l_r.at[me], who)

    loop(me + 1, n, lambda who: l_copy(who).start())

    for g in range(KV):
        for h in range(GROUP):
            at = (g * GROUP + h) * HEAD
            q = qbase[:, at:at + HEAD].astype(F32) + tn(qlow, qup[:, at:at + HEAD])
            qs[g, h * T:(h + 1) * T, :] = q.astype(BF16)

    kall[me] = kc[...]
    vall[me] = vb[...]
    key_pos = lax.broadcasted_iota(jnp.int32, (T, rows), 0)
    row_pos = lax.broadcasted_iota(jnp.int32, (T, rows), 1) % T
    seen = key_pos <= row_pos

    def make_value(j):
        vall[j] = (vall[j].astype(F32) + tn(vlow_all[j], vup)).astype(BF16)

    def stats(j, first):
        for g in range(KV):
            cols = slice(g * HEAD, (g + 1) * HEAD)
            s = nt(kall[j, :, cols], qs[g]) * c2
            dp = nt(vall[j, :, cols], dos[g])
            if first:
                s = jnp.where(seen, s, NEG)
                new = jnp.max(s, axis=0, keepdims=True)
                e = jnp.exp2(s - new)
                tot[g] = jnp.sum(e, axis=0, keepdims=True)
                wei[g] = jnp.sum(e * dp, axis=0, keepdims=True)
            else:
                old = top[g]
                new = jnp.maximum(old, jnp.max(s, axis=0, keepdims=True))
                e = jnp.exp2(s - new)
                decay = jnp.exp2(old - new)
                tot[g] = tot[g] * decay + jnp.sum(e, axis=0, keepdims=True)
                wei[g] = wei[g] * decay + jnp.sum(e * dp, axis=0, keepdims=True)
            top[g] = new

    make_value(me)
    stats(me, True)

    def stats_step(i):
        j = me - i
        to_seq(kc, kall.at[j], k_s.at[j], k_r.at[j], j).wait_recv()
        to_seq(vb, vall.at[j], v_s.at[j], v_r.at[j], j).wait_recv()
        to_seq(vlow_all.at[j], vlow_all.at[j], l_s.at[j], l_r.at[j], j).wait_recv()
        make_value(j)
        stats(j, False)

    loop(1, me + 1, stats_step)

    for g in range(KV):
        total = tot[g]
        top[g] = top[g] + jnp.log2(total)
        wei[g] = wei[g] / total

    def grads(j, first):
        part = jnp.zeros((RANK, T), F32)
        for g in range(KV):
            cols = slice(g * HEAD, (g + 1) * HEAD)
            key = kall[j, :, cols]
            s = nt(key, qs[g]) * c2
            dp = nt(vall[j, :, cols], dos[g])
            if first:
                s = jnp.where(seen, s, NEG)
            p = jnp.exp2(s - top[g])
            ds = (p * (dp - wei[g])).astype(BF16)
            dq = tn(key, ds)
            dv = nn(p.astype(BF16), dos[g]).astype(BF16)
            part = part + nt(vup[:, cols], dv)
            vu = nn(vlow_all[j], dv)
            if first:
                dqt[g] = dq
                vug[g] = vu
            else:
                dqt[g] += dq
                vug[g] += vu
        vgs[j] = part

    grads(me, True)

    def g_copy(j):
        return to_seq(vgs.at[j], vgx.at[me], g_s.at[j], g_r.at[me], j)

    def grads_step(i):
        j = me - i
        grads(j, False)
        g_copy(j).start()

    loop(1, me + 1, grads_step)

    qg = jnp.zeros((RANK, T), F32)
    for g in range(KV):
        for h in range(GROUP):
            at = (g * GROUP + h) * HEAD
            dq = (dqt[g, :, h * T:(h + 1) * T] * scale).astype(BF16)
            qg = qg + nn(qup[:, at:at + HEAD], dq)
            quw[:, at:at + HEAD] = nt(qlow, dq)

    def g_in(src):
        to_seq(vgs.at[src], vgx.at[src], g_s.at[src], g_r.at[src], src).wait_recv()

    loop(me + 1, n, g_in)
    vg = lax.fori_loop(me + 1, n, lambda s, acc: acc + vgx[s], vgs[me])
    gx[t] = jnp.concatenate([qg, vg], axis=0)

    def y_copy(who):
        return to_tp(gx.at[t], gx.at[t], y_s.at[who], y_r.at[t], who)

    def y_in(who):
        return to_tp(gx.at[who], gx.at[who], y_s.at[who], y_r.at[who], who)

    loop(1, m, lambda d: y_copy(lax.rem(t + d, m)).start())
    loop(1, m, lambda d: y_in(lax.rem(t + d, m)).wait_recv())
    lg = gx[0]
    for i in range(1, m):
        lg = lg + gx[i]
    dg = nn(lg.astype(BF16), hidden[...])

    outs = []
    for k in range(DL // HEAD):
        outs.append((dg[:RANK, k * HEAD:(k + 1) * HEAD], o_qd, o_qds, qdn, k))
    for k in range(DL // HEAD):
        outs.append((dg[RANK:, k * HEAD:(k + 1) * HEAD], o_vd, o_vds, vdn, k))
    for k in range(KV * GROUP):
        outs.append((quw[:, k * HEAD:(k + 1) * HEAD], o_qu, o_qus, qun, k))
    for k in range(KV):
        outs.append((vug[k], o_vu, o_vus, vun, k))
    for i in range(n * per):
        if i < units:
            pack[i // per, i % per] = outs[i][0].astype(BF16)
        else:
            pack[i // per, i % per] = jnp.zeros((RANK, HEAD), BF16)

    def r_copy(who):
        return to_seq(pack.at[who], rsx.at[me], r_s.at[who], r_r.at[me], who)

    def r_in(src):
        return to_seq(pack.at[src], rsx.at[src], r_s.at[src], r_r.at[src], src)

    loop(1, n, lambda d: r_copy(lax.rem(me + d, n)).start())
    rsx[me] = pack[me]
    loop(1, n, lambda d: r_in(lax.rem(me + d, n)).wait_recv())
    total = rsx[0].astype(F32)
    for i in range(1, n):
        total = total + rsx[i].astype(F32)
    agx[me] = total.astype(BF16)

    def a_copy(who):
        return to_seq(agx.at[me], agx.at[me], a_s.at[who], a_r.at[me], who)

    def a_in(src):
        return to_seq(agx.at[src], agx.at[src], a_s.at[src], a_r.at[src], src)

    loop(1, n, lambda d: a_copy(lax.rem(me + d, n)).start())
    loop(1, n, lambda d: a_in(lax.rem(me + d, n)).wait_recv())
    for i in range(units):
        _, mean, sigma, noise, k = outs[i]
        cols = slice(k * HEAD, (k + 1) * HEAD)
        value = agx[i // per, i % per].astype(F32)
        mean[:, cols] = value
        sigma[:, cols] = value * noise[:, cols]

    def drain_later(who):
        k_copy(who).wait_send()
        v_copy(who).wait_send()
        l_copy(who).wait_send()

    loop(me + 1, n, drain_later)
    loop(0, me, lambda j: g_copy(j).wait_send())

    def drain_tp(d):
        who = lax.rem(t + d, m)
        x_copy(who).wait_send()
        y_copy(who).wait_send()

    loop(1, m, drain_tp)

    def drain_seq(d):
        who = lax.rem(me + d, n)
        r_copy(who).wait_send()
        a_copy(who).wait_send()

    loop(1, n, drain_seq)


def solution(mesh):
    n = mesh.shape["seq"]
    m = mesh.shape["tp"]

    def step(*args):
        hidden, qbase, kc = args[:3]
        T, DL = hidden.shape
        QL, KL = qbase.shape[1], kc.shape[1]
        KV = KL // HEAD
        rows = GROUP * T
        units = (2 * DL + QL + KL) // HEAD
        per = -(-units // n)
        shape = lambda cols: jax.ShapeDtypeStruct((RANK, cols), F32)
        vmem = pl.BlockSpec(memory_space=pltpu.VMEM)
        sem = pltpu.SemaphoreType.DMA
        return tuple(pl.pallas_call(
            functools.partial(kernel, n, m, units, per),
            out_shape=[shape(c) for c in (DL, DL, QL, QL, DL, DL, KL, KL)],
            in_specs=[vmem] * 17,
            out_specs=[vmem] * 8,
            scratch_shapes=[
                pltpu.VMEM((n, T, KL), BF16),
                pltpu.VMEM((n, T, KL), BF16),
                pltpu.VMEM((n, RANK, T), BF16),
                pltpu.VMEM((m, 2 * RANK, T), F32),
                pltpu.VMEM((m, 2 * RANK, T), F32),
                pltpu.VMEM((KV, rows, HEAD), BF16),
                pltpu.VMEM((KV, rows, HEAD), BF16),
                pltpu.VMEM((KV, 1, rows), F32),
                pltpu.VMEM((KV, 1, rows), F32),
                pltpu.VMEM((KV, 1, rows), F32),
                pltpu.VMEM((KV, HEAD, rows), F32),
                pltpu.VMEM((n, RANK, T), F32),
                pltpu.VMEM((n, RANK, T), F32),
                pltpu.VMEM((KV, RANK, HEAD), F32),
                pltpu.VMEM((RANK, QL), F32),
                pltpu.VMEM((n, per, RANK, HEAD), BF16),
                pltpu.VMEM((n, per, RANK, HEAD), BF16),
                pltpu.VMEM((n, per, RANK, HEAD), BF16),
            ] + [sem((k,)) for k in (n, n, n, n, n, n, m, m, m, m, n, n, n, n, n, n)],
            compiler_params=pltpu.CompilerParams(
                collective_id=0, has_side_effects=True, vmem_limit_bytes=48 * 1024 * 1024
            ),
            cost_estimate=pl.CostEstimate(
                flops=14 * rows * KV * n * T * HEAD // 2,
                bytes_accessed=8 * 1024 * 1024,
                transcendentals=rows * KV * n * T,
            ),
        )(*args))

    wide = P("seq", "tp")
    flat = P(None, "tp")
    return jax.shard_map(
        step,
        mesh=mesh,
        in_specs=(wide,) * 5 + (flat,) * 12,
        out_specs=(flat,) * 8,
        check_vma=False,
    )
```

```python
import functools
import math

import jax
import jax.numpy as jnp
from jax import lax
from jax.experimental import pallas as pl
from jax.experimental.pallas import tpu as pltpu
from jax.sharding import PartitionSpec as P

HEAD = 128
RANK = 16
GROUP = 4
F32 = jnp.float32
BF16 = jnp.bfloat16
NEG = -1e30


def nt(a, b):
    return lax.dot_general(a, b, (((1,), (1,)), ((), ())), preferred_element_type=F32)


def tn(a, b):
    return lax.dot_general(a, b, (((0,), (0,)), ((), ())), preferred_element_type=F32)


def nn(a, b):
    return jnp.dot(a, b, preferred_element_type=F32)


def kernel(
    n, m, units, per, X, *refs,
):
    sources = refs[:17]
    held = refs[25:42]
    loaded = refs[-1]
    hidden, qbase, kc, vb, og, qdm, qds, qdn, qum, qus, qun, vdm, vds, vdn, vum, vus, vun = held
    kc, vb = sources[2:4]
    (
        o_qd, o_qds, o_qu, o_qus, o_vd, o_vds, o_vu, o_vus,
    ) = refs[17:25]
    (
    kall, vall, vval, vlow_all, lowx, gx, qs, dos, top, tot, wei, dqt, vgs, vgx, vug, quw, pack, rsx, agx,
    k_s, k_r, v_s, v_r, l_s, l_r, x_s, x_r, y_s, y_r, g_s, g_r, r_s, r_r, a_s, a_r,
    ) = refs[42:-1]
    T, DL = hidden.shape
    KV = kc.shape[1] // HEAD
    rows = GROUP * T
    scale = HEAD ** -0.5
    c2 = scale * math.log2(math.e)
    me = lax.axis_index("seq")
    t = lax.axis_index("tp")

    def to_seq(src, dst, ss, rs, who):
        return pltpu.make_async_remote_copy(
            src_ref=src, dst_ref=dst, send_sem=ss, recv_sem=rs,
            device_id=(who, t), device_id_type=pl.DeviceIdType.MESH,
        )

    def to_tp(src, dst, ss, rs, who):
        return pltpu.make_async_remote_copy(
            src_ref=src, dst_ref=dst, send_sem=ss, recv_sem=rs,
            device_id=(me, who), device_id_type=pl.DeviceIdType.MESH,
        )

    def loop(lo, hi, body):
        def step(i, c):
            body(i)
            return c
        lax.fori_loop(lo, hi, step, 0)

    def load(i):
        dst = held[i]
        if i == 2:
            dst = kall.at[me]
        if i == 3:
            dst = vall.at[me]
        return pltpu.make_async_copy(sources[i], dst, loaded.at[i])

    order = (0, 5, 6, 7, 11, 12, 13, 4, 1, 8, 9, 10, 14, 15, 16, 2, 3)
    for i in order:
        load(i).start()

    barrier = pltpu.get_barrier_semaphore()

    def greet_seq(d):
        pl.semaphore_signal(
            barrier, inc=1, device_id=(lax.rem(me + d, n), t),
            device_id_type=pl.DeviceIdType.MESH,
        )

    def greet_tp(d):
        pl.semaphore_signal(
            barrier, inc=1, device_id=(me, lax.rem(t + d, m)),
            device_id_type=pl.DeviceIdType.MESH,
        )

    loop(1, n, greet_seq)
    loop(1, m, greet_tp)
    pl.semaphore_wait(barrier, n + m - 2)

    x = lax.rem(me, X)
    plane = me - x

    def kv(part, j, who, slot, own=False):
        if part == 0:
            return to_seq(kc if own else kall.at[j], kall.at[j], k_s.at[j, slot], k_r.at[j], who)
        return to_seq(vb if own else vall.at[j], vall.at[j], v_s.at[j, slot], v_r.at[j], who)

    def hand_on(j, part, own, act):
        @pl.when(me + X < n)
        def _():
            act(kv(part, j, me + X, 0, own))

        def across(d):
            other = lax.rem(x + d, X)

            @pl.when(plane + other > j)
            def _():
                act(kv(part, j, plane + other, 1 + other, own))

        loop(1, X, across)

    for part in range(2):
        hand_on(me, part, True, lambda c: c.start())

    for i in order[:7]:
        load(i).wait()
    qdown = (qdm[...] + qds[...] * qdn[...]).astype(BF16)
    vdown = (vdm[...] + vds[...] * vdn[...]).astype(BF16)
    lowx[t] = jnp.concatenate([nt(qdown, hidden[...]), nt(vdown, hidden[...])], axis=0)

    def x_copy(who):
        return to_tp(lowx.at[t], lowx.at[t], x_s.at[who], x_r.at[t], who)

    def x_in(who):
        return to_tp(lowx.at[who], lowx.at[who], x_s.at[who], x_r.at[who], who)

    loop(1, m, lambda d: x_copy(lax.rem(t + d, m)).start())
    for i in order[7:]:
        load(i).wait()
    qup = (qum[...] + qus[...] * qun[...]).astype(BF16)
    vup = (vum[...] + vus[...] * vun[...]).astype(BF16)
    for g in range(KV):
        for h in range(GROUP):
            at = (g * GROUP + h) * HEAD
            dos[g, h * T:(h + 1) * T, :] = og[:, at:at + HEAD]
    loop(1, m, lambda d: x_in(lax.rem(t + d, m)).wait_recv())
    low = lowx[0]
    for i in range(1, m):
        low = low + lowx[i]
    low = low.astype(BF16)
    qlow = low[:RANK]
    vlow = low[RANK:]
    vlow_all[me] = vlow

    def l_copy(who):
        return to_seq(vlow_all.at[me], vlow_all.at[me], l_s.at[who], l_r.at[me], who)

    loop(me + 1, n, lambda who: l_copy(who).start())

    for g in range(KV):
        for h in range(GROUP):
            at = (g * GROUP + h) * HEAD
            q = qbase[:, at:at + HEAD].astype(F32) + tn(qlow, qup[:, at:at + HEAD])
            qs[g, h * T:(h + 1) * T, :] = q.astype(BF16)

    key_pos = lax.broadcasted_iota(jnp.int32, (T, rows), 0)
    row_pos = lax.broadcasted_iota(jnp.int32, (T, rows), 1) % T
    seen = key_pos <= row_pos

    def make_value(j):
        vval[j] = (vall[j].astype(F32) + tn(vlow_all[j], vup)).astype(BF16)

    def stats(j, first):
        for g in range(KV):
            cols = slice(g * HEAD, (g + 1) * HEAD)
            s = nt(kall[j, :, cols], qs[g]) * c2
            dp = nt(vval[j, :, cols], dos[g])
            if first:
                s = jnp.where(seen, s, NEG)
                new = jnp.max(s, axis=0, keepdims=True)
                e = jnp.exp2(s - new)
                tot[g] = jnp.sum(e, axis=0, keepdims=True)
                wei[g] = jnp.sum(e * dp, axis=0, keepdims=True)
            else:
                old = top[g]
                new = jnp.maximum(old, jnp.max(s, axis=0, keepdims=True))
                e = jnp.exp2(s - new)
                decay = jnp.exp2(old - new)
                tot[g] = tot[g] * decay + jnp.sum(e, axis=0, keepdims=True)
                wei[g] = wei[g] * decay + jnp.sum(e * dp, axis=0, keepdims=True)
            top[g] = new

    make_value(me)
    stats(me, True)

    def arrive(j):
        to_seq(vlow_all.at[j], vlow_all.at[j], l_s.at[j], l_r.at[j], j).wait_recv()
        make_value(j)
        stats(j, False)

    def from_column(i):
        j = me - i * X
        for part in range(2):
            kv(part, j, me, 0).wait_recv()
            hand_on(j, part, False, lambda c: c.start())
        arrive(j)

    def from_across(j):
        @pl.when(lax.rem(j, X) != x)
        def _():
            for part in range(2):
                kv(part, j, me, 0).wait_recv()
            arrive(j)

    loop(plane, me, from_across)
    loop(1, me // X + 1, from_column)
    loop(1, plane + 1, lambda i: from_across(plane - i))

    for g in range(KV):
        total = tot[g]
        top[g] = top[g] + jnp.log2(total)
        wei[g] = wei[g] / total

    def grads(j, first):
        part = jnp.zeros((RANK, T), F32)
        for g in range(KV):
            cols = slice(g * HEAD, (g + 1) * HEAD)
            key = kall[j, :, cols]
            s = nt(key, qs[g]) * c2
            dp = nt(vval[j, :, cols], dos[g])
            if first:
                s = jnp.where(seen, s, NEG)
            p = jnp.exp2(s - top[g])
            ds = (p * (dp - wei[g])).astype(BF16)
            dq = tn(key, ds)
            dv = nn(p.astype(BF16), dos[g]).astype(BF16)
            part = part + nt(vup[:, cols], dv)
            vu = nn(vlow_all[j], dv)
            if first:
                dqt[g] = dq
                vug[g] = vu
            else:
                dqt[g] += dq
                vug[g] += vu
        vgs[j] = part

    grads(me, True)

    def g_copy(j):
        return to_seq(vgs.at[j], vgx.at[me], g_s.at[j], g_r.at[me], j)

    def grads_step(i):
        j = me - i
        grads(j, False)
        g_copy(j).start()

    loop(1, me + 1, grads_step)

    qg = jnp.zeros((RANK, T), F32)
    for g in range(KV):
        for h in range(GROUP):
            at = (g * GROUP + h) * HEAD
            dq = (dqt[g, :, h * T:(h + 1) * T] * scale).astype(BF16)
            qg = qg + nn(qup[:, at:at + HEAD], dq)
            quw[:, at:at + HEAD] = nt(qlow, dq)

    def g_in(src):
        to_seq(vgs.at[src], vgx.at[src], g_s.at[src], g_r.at[src], src).wait_recv()

    loop(me + 1, n, g_in)
    vg = lax.fori_loop(me + 1, n, lambda s, acc: acc + vgx[s], vgs[me])
    gx[t] = jnp.concatenate([qg, vg], axis=0)

    def y_copy(who):
        return to_tp(gx.at[t], gx.at[t], y_s.at[who], y_r.at[t], who)

    def y_in(who):
        return to_tp(gx.at[who], gx.at[who], y_s.at[who], y_r.at[who], who)

    loop(1, m, lambda d: y_copy(lax.rem(t + d, m)).start())
    loop(1, m, lambda d: y_in(lax.rem(t + d, m)).wait_recv())
    lg = gx[0]
    for i in range(1, m):
        lg = lg + gx[i]
    dg = nn(lg.astype(BF16), hidden[...])

    outs = []
    for k in range(DL // HEAD):
        outs.append((dg[:RANK, k * HEAD:(k + 1) * HEAD], o_qd, o_qds, qdn, k))
    for k in range(DL // HEAD):
        outs.append((dg[RANK:, k * HEAD:(k + 1) * HEAD], o_vd, o_vds, vdn, k))
    for k in range(KV * GROUP):
        outs.append((quw[:, k * HEAD:(k + 1) * HEAD], o_qu, o_qus, qun, k))
    for k in range(KV):
        outs.append((vug[k], o_vu, o_vus, vun, k))
    for i in range(n * per):
        if i < units:
            pack[i // per, i % per] = outs[i][0].astype(BF16)
        else:
            pack[i // per, i % per] = jnp.zeros((RANK, HEAD), BF16)

    def r_copy(who):
        return to_seq(pack.at[who], rsx.at[me], r_s.at[who], r_r.at[me], who)

    def r_in(src):
        return to_seq(pack.at[src], rsx.at[src], r_s.at[src], r_r.at[src], src)

    loop(1, n, lambda d: r_copy(lax.rem(me + d, n)).start())
    rsx[me] = pack[me]
    loop(1, n, lambda d: r_in(lax.rem(me + d, n)).wait_recv())
    total = rsx[0].astype(F32)
    for i in range(1, n):
        total = total + rsx[i].astype(F32)
    agx[me] = total.astype(BF16)

    def a_copy(who):
        return to_seq(agx.at[me], agx.at[me], a_s.at[who], a_r.at[me], who)

    def a_in(src):
        return to_seq(agx.at[src], agx.at[src], a_s.at[src], a_r.at[src], src)

    loop(1, n, lambda d: a_copy(lax.rem(me + d, n)).start())
    loop(1, n, lambda d: a_in(lax.rem(me + d, n)).wait_recv())
    for i in range(units):
        _, mean, sigma, noise, k = outs[i]
        cols = slice(k * HEAD, (k + 1) * HEAD)
        value = agx[i // per, i % per].astype(F32)
        mean[:, cols] = value
        sigma[:, cols] = value * noise[:, cols]

    def drain_later(who):
        l_copy(who).wait_send()

    loop(me + 1, n, drain_later)
    loop(0, me, lambda j: g_copy(j).wait_send())
    for part in range(2):
        hand_on(me, part, True, lambda c: c.wait_send())
        loop(1, me // X + 1, lambda i: hand_on(me - i * X, part, False, lambda c: c.wait_send()))

    def drain_tp(d):
        who = lax.rem(t + d, m)
        x_copy(who).wait_send()
        y_copy(who).wait_send()

    loop(1, m, drain_tp)

    def drain_seq(d):
        who = lax.rem(me + d, n)
        r_copy(who).wait_send()
        a_copy(who).wait_send()

    loop(1, n, drain_seq)


def hand_out(*refs):
    count = (len(refs) - 1) // 2
    sems = refs[-1]
    copies = [
        pltpu.make_async_copy(refs[i], refs[count + i], sems.at[i]) for i in range(count)
    ]
    for c in copies:
        c.start()
    for c in copies:
        c.wait()


def solution(mesh):
    n = mesh.shape["seq"]
    m = mesh.shape["tp"]

    def step(*args):
        hidden, qbase, kc = args[:3]
        T, DL = hidden.shape
        QL, KL = qbase.shape[1], kc.shape[1]
        KV = KL // HEAD
        rows = GROUP * T
        units = (2 * DL + QL + KL) // HEAD
        per = -(-units // n)
        shape = lambda cols: jax.ShapeDtypeStruct((RANK, cols), F32)
        X = 1
        while 2 * (2 * X) ** 2 <= n:
            X *= 2
        hbm = pl.BlockSpec(memory_space=pltpu.HBM)
        vmem = pl.BlockSpec(memory_space=pltpu.VMEM)
        sem = pltpu.SemaphoreType.DMA
        outs = pl.pallas_call(
            functools.partial(kernel, n, m, units, per, X),
            out_shape=[shape(c) for c in (DL, DL, QL, QL, DL, DL, KL, KL)],
            in_specs=[hbm] * 17,
            out_specs=[vmem] * 8,
            scratch_shapes=[pltpu.VMEM(a.shape, a.dtype) for a in args] + [
                pltpu.VMEM((n, T, KL), BF16),
                pltpu.VMEM((n, T, KL), BF16),
                pltpu.VMEM((n, T, KL), BF16),
                pltpu.VMEM((n, RANK, T), BF16),
                pltpu.VMEM((m, 2 * RANK, T), F32),
                pltpu.VMEM((m, 2 * RANK, T), F32),
                pltpu.VMEM((KV, rows, HEAD), BF16),
                pltpu.VMEM((KV, rows, HEAD), BF16),
                pltpu.VMEM((KV, 1, rows), F32),
                pltpu.VMEM((KV, 1, rows), F32),
                pltpu.VMEM((KV, 1, rows), F32),
                pltpu.VMEM((KV, HEAD, rows), F32),
                pltpu.VMEM((n, RANK, T), F32),
                pltpu.VMEM((n, RANK, T), F32),
                pltpu.VMEM((KV, RANK, HEAD), F32),
                pltpu.VMEM((RANK, QL), F32),
                pltpu.VMEM((n, per, RANK, HEAD), BF16),
                pltpu.VMEM((n, per, RANK, HEAD), BF16),
                pltpu.VMEM((n, per, RANK, HEAD), BF16),
            ] + [sem((n, 1 + X)), sem((n,)), sem((n, 1 + X)), sem((n,))]
            + [sem((k,)) for k in (n, n, m, m, m, m, n, n, n, n, n, n, 17)],
            compiler_params=pltpu.CompilerParams(
                collective_id=0, has_side_effects=True, vmem_limit_bytes=63 * 1024 * 1024
            ),
            cost_estimate=pl.CostEstimate(
                flops=14 * rows * KV * n * T * HEAD // 2,
                bytes_accessed=8 * 1024 * 1024,
                transcendentals=rows * KV * n * T,
            ),
        )(*args)
        return tuple(pl.pallas_call(
            hand_out,
            out_shape=[jax.ShapeDtypeStruct(a.shape, a.dtype) for a in outs],
            in_specs=[hbm] * 8,
            out_specs=[hbm] * 8,
            scratch_shapes=[sem((8,))],
            compiler_params=pltpu.CompilerParams(vmem_limit_bytes=63 * 1024 * 1024),
        )(*outs))

    wide = P("seq", "tp")
    flat = P(None, "tp")
    return jax.shard_map(
        step,
        mesh=mesh,
        in_specs=(wide,) * 5 + (flat,) * 12,
        out_specs=(flat,) * 8,
        check_vma=False,
    )
```

```python
import functools
import math

import jax
import jax.numpy as jnp
from jax import lax
from jax.experimental import pallas as pl
from jax.experimental.pallas import tpu as pltpu
from jax.sharding import PartitionSpec as P

HEAD = 128
RANK = 16
GROUP = 4
F32 = jnp.float32
BF16 = jnp.bfloat16
NEG = -1e30


def nt(a, b):
    return lax.dot_general(a, b, (((1,), (1,)), ((), ())), preferred_element_type=F32)


def tn(a, b):
    return lax.dot_general(a, b, (((0,), (0,)), ((), ())), preferred_element_type=F32)


def nn(a, b):
    return jnp.dot(a, b, preferred_element_type=F32)


def kernel(
    n, m, up_per, down_per, keep, X, *refs,
):
    sources = refs[:17]
    held = refs[19:36]
    loaded = refs[-1]
    hidden, qbase, kc, vb, og, qdm, qds, qdn, qum, qus, qun, vdm, vds, vdn, vum, vus, vun = held
    kc, vb = sources[2:4]
    up_out, down_out = refs[17:19]
    (
    kall, vall, vval, vlow_all, lowx, gx, qs, dos, top, tot, wei, dqt, vgs, vgx, vug, quw, up_pack, up_rsx, up_agx, down_pack, down_rsx, down_agx, s_kept, dp_kept,
    k_s, k_r, v_s, v_r, l_s, l_r, x_s, x_r, y_s, y_r, g_s, g_r, ur_s, ur_r, ua_s, ua_r, dr_s, dr_r, da_s, da_r,
    ) = refs[36:-1]
    T, DL = hidden.shape
    KV = kc.shape[1] // HEAD
    rows = GROUP * T
    scale = HEAD ** -0.5
    c2 = scale * math.log2(math.e)
    me = lax.axis_index("seq")
    t = lax.axis_index("tp")

    def to_seq(src, dst, ss, rs, who):
        return pltpu.make_async_remote_copy(
            src_ref=src, dst_ref=dst, send_sem=ss, recv_sem=rs,
            device_id=(who, t), device_id_type=pl.DeviceIdType.MESH,
        )

    def to_tp(src, dst, ss, rs, who):
        return pltpu.make_async_remote_copy(
            src_ref=src, dst_ref=dst, send_sem=ss, recv_sem=rs,
            device_id=(me, who), device_id_type=pl.DeviceIdType.MESH,
        )

    def loop(lo, hi, body):
        def step(i, c):
            body(i)
            return c
        lax.fori_loop(lo, hi, step, 0)

    def load(i):
        dst = held[i]
        if i == 2:
            dst = kall.at[me]
        if i == 3:
            dst = vall.at[me]
        return pltpu.make_async_copy(sources[i], dst, loaded.at[i])

    order = (0, 5, 6, 7, 11, 12, 13, 4, 1, 8, 9, 10, 14, 15, 16, 2, 3)
    for i in order:
        load(i).start()

    barrier = pltpu.get_barrier_semaphore()

    def greet_seq(d):
        pl.semaphore_signal(
            barrier, inc=1, device_id=(lax.rem(me + d, n), t),
            device_id_type=pl.DeviceIdType.MESH,
        )

    def greet_tp(d):
        pl.semaphore_signal(
            barrier, inc=1, device_id=(me, lax.rem(t + d, m)),
            device_id_type=pl.DeviceIdType.MESH,
        )

    loop(1, n, greet_seq)
    loop(1, m, greet_tp)
    pl.semaphore_wait(barrier, n + m - 2)

    x = lax.rem(me, X)
    plane = me - x

    def kv(part, j, who, slot, own=False):
        if part == 0:
            return to_seq(kc if own else kall.at[j], kall.at[j], k_s.at[j, slot], k_r.at[j], who)
        return to_seq(vb if own else vall.at[j], vall.at[j], v_s.at[j, slot], v_r.at[j], who)

    def hand_on(j, part, own, act):
        @pl.when(me + X < n)
        def _():
            act(kv(part, j, me + X, 0, own))

        def across(d):
            other = lax.rem(x + d, X)

            @pl.when(plane + other > j)
            def _():
                act(kv(part, j, plane + other, 1 + other, own))

        loop(1, X, across)

    for part in range(2):
        hand_on(me, part, True, lambda c: c.start())

    for i in order[:7]:
        load(i).wait()
    qdown = (qdm[...] + qds[...] * qdn[...]).astype(BF16)
    vdown = (vdm[...] + vds[...] * vdn[...]).astype(BF16)
    lowx[t] = jnp.concatenate([nt(qdown, hidden[...]), nt(vdown, hidden[...])], axis=0)

    def x_copy(who):
        return to_tp(lowx.at[t], lowx.at[t], x_s.at[who], x_r.at[t], who)

    def x_in(who):
        return to_tp(lowx.at[who], lowx.at[who], x_s.at[who], x_r.at[who], who)

    loop(1, m, lambda d: x_copy(lax.rem(t + d, m)).start())
    for i in order[7:]:
        load(i).wait()
    qup = (qum[...] + qus[...] * qun[...]).astype(BF16)
    vup = (vum[...] + vus[...] * vun[...]).astype(BF16)
    for g in range(KV):
        for h in range(GROUP):
            at = (g * GROUP + h) * HEAD
            dos[g, h * T:(h + 1) * T, :] = og[:, at:at + HEAD]
    loop(1, m, lambda d: x_in(lax.rem(t + d, m)).wait_recv())
    low = lowx[0]
    for i in range(1, m):
        low = low + lowx[i]
    low = low.astype(BF16)
    qlow = low[:RANK]
    vlow = low[RANK:]
    vlow_all[me] = vlow

    def l_copy(who):
        return to_seq(vlow_all.at[me], vlow_all.at[me], l_s.at[who], l_r.at[me], who)

    loop(me + 1, n, lambda who: l_copy(who).start())

    for g in range(KV):
        for h in range(GROUP):
            at = (g * GROUP + h) * HEAD
            q = qbase[:, at:at + HEAD].astype(F32) + tn(qlow, qup[:, at:at + HEAD])
            qs[g, h * T:(h + 1) * T, :] = q.astype(BF16)

    key_pos = lax.broadcasted_iota(jnp.int32, (T, rows), 0)
    row_pos = lax.broadcasted_iota(jnp.int32, (T, rows), 1) % T
    seen = key_pos <= row_pos

    def make_value(j):
        vval[j] = (vall[j].astype(F32) + tn(vlow_all[j], vup)).astype(BF16)

    def stats(j, first):
        for g in range(KV):
            cols = slice(g * HEAD, (g + 1) * HEAD)
            s = nt(kall[j, :, cols], qs[g]) * c2
            dp = nt(vval[j, :, cols], dos[g])
            if first:
                s = jnp.where(seen, s, NEG)
            if keep:
                s_kept[j, g] = s
                dp_kept[j, g] = dp
            if first:
                new = jnp.max(s, axis=0, keepdims=True)
                e = jnp.exp2(s - new)
                tot[g] = jnp.sum(e, axis=0, keepdims=True)
                wei[g] = jnp.sum(e * dp, axis=0, keepdims=True)
            else:
                old = top[g]
                new = jnp.maximum(old, jnp.max(s, axis=0, keepdims=True))
                e = jnp.exp2(s - new)
                decay = jnp.exp2(old - new)
                tot[g] = tot[g] * decay + jnp.sum(e, axis=0, keepdims=True)
                wei[g] = wei[g] * decay + jnp.sum(e * dp, axis=0, keepdims=True)
            top[g] = new

    make_value(me)
    stats(me, True)

    def arrive(j):
        to_seq(vlow_all.at[j], vlow_all.at[j], l_s.at[j], l_r.at[j], j).wait_recv()
        make_value(j)
        stats(j, False)

    def from_column(i):
        j = me - i * X
        for part in range(2):
            kv(part, j, me, 0).wait_recv()
            hand_on(j, part, False, lambda c: c.start())
        arrive(j)

    def from_across(j):
        @pl.when(lax.rem(j, X) != x)
        def _():
            for part in range(2):
                kv(part, j, me, 0).wait_recv()
            arrive(j)

    loop(plane, me, from_across)
    loop(1, me // X + 1, from_column)
    loop(1, plane + 1, lambda i: from_across(plane - i))

    for g in range(KV):
        total = tot[g]
        top[g] = top[g] + jnp.log2(total)
        wei[g] = wei[g] / total

    dqt[...] = jnp.zeros_like(dqt)
    vug[...] = jnp.zeros_like(vug)

    def grads(j, own):
        part = jnp.zeros((RANK, T), F32)
        for g in range(KV):
            cols = slice(g * HEAD, (g + 1) * HEAD)
            key = kall[j, :, cols]
            if keep:
                s = s_kept[j, g]
                dp = dp_kept[j, g]
            else:
                s = nt(key, qs[g]) * c2
                dp = nt(vval[j, :, cols], dos[g])
                if own:
                    s = jnp.where(seen, s, NEG)
            p = jnp.exp2(s - top[g])
            ds = (p * (dp - wei[g])).astype(BF16)
            dqt[g] += tn(key, ds)
            dv = nn(p.astype(BF16), dos[g]).astype(BF16)
            part = part + nt(vup[:, cols], dv)
            vug[g] += nn(vlow_all[j], dv)
        vgs[j] = part

    def g_copy(j):
        return to_seq(vgs.at[j], vgx.at[me], g_s.at[j], g_r.at[me], j)

    def grads_step(j):
        grads(j, False)
        g_copy(j).start()

    loop(0, me, grads_step)
    grads(me, True)

    qg = jnp.zeros((RANK, T), F32)
    for g in range(KV):
        for h in range(GROUP):
            at = (g * GROUP + h) * HEAD
            dq = (dqt[g, :, h * T:(h + 1) * T] * scale).astype(BF16)
            qg = qg + nn(qup[:, at:at + HEAD], dq)
            quw[:, at:at + HEAD] = nt(qlow, dq)

    def deal(tiles, per, pack):
        for i in range(n * per):
            pack[i // per, i % per] = (
                tiles[i].astype(BF16) if i < len(tiles) else jnp.zeros((RANK, HEAD), BF16)
            )

    def others(act):
        loop(1, n, lambda d: act(lax.rem(me + d, n)))

    def r_copy(pack, rsx, ss, rs, who):
        return to_seq(pack.at[who], rsx.at[me], ss.at[who], rs.at[me], who)

    def a_copy(agx, ss, rs, who):
        return to_seq(agx.at[me], agx.at[me], ss.at[who], rs.at[me], who)

    def reduce_in(pack, rsx, agx, ss, rs):
        rsx[me] = pack[me]
        others(lambda w: to_seq(pack.at[w], rsx.at[w], ss.at[w], rs.at[w], w).wait_recv())
        total = rsx[0].astype(F32)
        for i in range(1, n):
            total = total + rsx[i].astype(F32)
        agx[me] = total.astype(BF16)

    def gather_in(agx, ss, rs):
        others(lambda w: to_seq(agx.at[w], agx.at[w], ss.at[w], rs.at[w], w).wait_recv())

    deal(
        [quw[:, k * HEAD:(k + 1) * HEAD] for k in range(KV * GROUP)] + [vug[k] for k in range(KV)],
        up_per, up_pack,
    )
    others(lambda w: r_copy(up_pack, up_rsx, ur_s, ur_r, w).start())

    def g_in(src):
        to_seq(vgs.at[src], vgx.at[src], g_s.at[src], g_r.at[src], src).wait_recv()

    loop(me + 1, n, g_in)
    vg = lax.fori_loop(me + 1, n, lambda s, acc: acc + vgx[s], vgs[me])
    gx[t] = jnp.concatenate([qg, vg], axis=0)

    def y_copy(who):
        return to_tp(gx.at[t], gx.at[t], y_s.at[who], y_r.at[t], who)

    def y_in(who):
        return to_tp(gx.at[who], gx.at[who], y_s.at[who], y_r.at[who], who)

    loop(1, m, lambda d: y_copy(lax.rem(t + d, m)).start())
    loop(1, m, lambda d: y_in(lax.rem(t + d, m)).wait_recv())
    lg = gx[0]
    for i in range(1, m):
        lg = lg + gx[i]
    dg = nn(lg.astype(BF16), hidden[...])

    deal(
        [dg[:RANK, k * HEAD:(k + 1) * HEAD] for k in range(DL // HEAD)]
        + [dg[RANK:, k * HEAD:(k + 1) * HEAD] for k in range(DL // HEAD)],
        down_per, down_pack,
    )
    others(lambda w: r_copy(down_pack, down_rsx, dr_s, dr_r, w).start())
    reduce_in(up_pack, up_rsx, up_agx, ur_s, ur_r)
    others(lambda w: a_copy(up_agx, ua_s, ua_r, w).start())
    reduce_in(down_pack, down_rsx, down_agx, dr_s, dr_r)
    others(lambda w: a_copy(down_agx, da_s, da_r, w).start())
    gather_in(up_agx, ua_s, ua_r)
    up_out[...] = up_agx[...]
    gather_in(down_agx, da_s, da_r)
    down_out[...] = down_agx[...]

    def drain_later(who):
        l_copy(who).wait_send()

    loop(me + 1, n, drain_later)
    loop(0, me, lambda j: g_copy(j).wait_send())
    for part in range(2):
        hand_on(me, part, True, lambda c: c.wait_send())
        loop(1, me // X + 1, lambda i: hand_on(me - i * X, part, False, lambda c: c.wait_send()))

    def drain_tp(d):
        who = lax.rem(t + d, m)
        x_copy(who).wait_send()
        y_copy(who).wait_send()

    loop(1, m, drain_tp)

    def drain_seq(d):
        who = lax.rem(me + d, n)
        r_copy(up_pack, up_rsx, ur_s, ur_r, who).wait_send()
        a_copy(up_agx, ua_s, ua_r, who).wait_send()
        r_copy(down_pack, down_rsx, dr_s, dr_r, who).wait_send()
        a_copy(down_agx, da_s, da_r, who).wait_send()

    loop(1, n, drain_seq)


def hand_out(*refs):
    up, down = refs[6 + 8:6 + 8 + 2]
    noises = refs[16:20]
    outs = refs[20:28]
    in_sem, out_sem = refs[28:]
    loads = [
        pltpu.make_async_copy(refs[i], refs[14 + i], in_sem.at[i]) for i in range(6)
    ]
    stores = [
        pltpu.make_async_copy(outs[i], refs[6 + i], out_sem.at[i]) for i in range(8)
    ]
    for c in loads:
        c.start()
    for c in loads:
        c.wait()
    per = (up.shape[1], down.shape[1])
    at = [0, 0]
    for which, i in ((1, 0), (1, 2), (0, 1), (0, 3)):
        for k in range(noises[i].shape[1] // HEAD):
            unit = at[which]
            at[which] += 1
            cols = slice(k * HEAD, (k + 1) * HEAD)
            value = (up, down)[which][unit // per[which], unit % per[which]].astype(F32)
            outs[2 * i][:, cols] = value
            outs[2 * i + 1][:, cols] = value * noises[i][:, cols]
        stores[2 * i].start()
        stores[2 * i + 1].start()
    for c in stores:
        c.wait()


def solution(mesh):
    n = mesh.shape["seq"]
    m = mesh.shape["tp"]

    def step(*args):
        hidden, qbase, kc = args[:3]
        T, DL = hidden.shape
        QL, KL = qbase.shape[1], kc.shape[1]
        KV = KL // HEAD
        rows = GROUP * T
        up_per = -(-(QL + KL) // (HEAD * n))
        down_per = -(-2 * DL // (HEAD * n))
        keep = n * KV * T * rows * 8 <= 36 * 1024 * 1024
        kept = (n, KV, T, rows) if keep else (1, 1, 8, HEAD)
        shape = lambda cols: jax.ShapeDtypeStruct((RANK, cols), F32)
        X = 1
        while 2 * (2 * X) ** 2 <= n:
            X *= 2
        hbm = pl.BlockSpec(memory_space=pltpu.HBM)
        vmem = pl.BlockSpec(memory_space=pltpu.VMEM)
        sem = pltpu.SemaphoreType.DMA
        outs = pl.pallas_call(
            functools.partial(kernel, n, m, up_per, down_per, keep, X),
            out_shape=[
                jax.ShapeDtypeStruct((n, up_per, RANK, HEAD), BF16),
                jax.ShapeDtypeStruct((n, down_per, RANK, HEAD), BF16),
            ],
            in_specs=[hbm] * 17,
            out_specs=[vmem] * 2,
            scratch_shapes=[pltpu.VMEM(a.shape, a.dtype) for a in args] + [
                pltpu.VMEM((n, T, KL), BF16),
                pltpu.VMEM((n, T, KL), BF16),
                pltpu.VMEM((n, T, KL), BF16),
                pltpu.VMEM((n, RANK, T), BF16),
                pltpu.VMEM((m, 2 * RANK, T), F32),
                pltpu.VMEM((m, 2 * RANK, T), F32),
                pltpu.VMEM((KV, rows, HEAD), BF16),
                pltpu.VMEM((KV, rows, HEAD), BF16),
                pltpu.VMEM((KV, 1, rows), F32),
                pltpu.VMEM((KV, 1, rows), F32),
                pltpu.VMEM((KV, 1, rows), F32),
                pltpu.VMEM((KV, HEAD, rows), F32),
                pltpu.VMEM((n, RANK, T), F32),
                pltpu.VMEM((n, RANK, T), F32),
                pltpu.VMEM((KV, RANK, HEAD), F32),
                pltpu.VMEM((RANK, QL), F32),
            ] + [pltpu.VMEM((n, up_per, RANK, HEAD), BF16)] * 3
            + [pltpu.VMEM((n, down_per, RANK, HEAD), BF16)] * 3 + [
                pltpu.VMEM(kept, F32),
                pltpu.VMEM(kept, F32),
            ] + [sem((n, 1 + X)), sem((n,)), sem((n, 1 + X)), sem((n,))]
            + [sem((k,)) for k in (n, n, m, m, m, m) + (n,) * 10 + (17,)],
            compiler_params=pltpu.CompilerParams(
                collective_id=0, has_side_effects=True, vmem_limit_bytes=63 * 1024 * 1024
            ),
            cost_estimate=pl.CostEstimate(
                flops=14 * rows * KV * n * T * HEAD // 2,
                bytes_accessed=8 * 1024 * 1024,
                transcendentals=rows * KV * n * T,
            ),
        )(*args)
        taken = tuple(outs) + (args[7], args[10], args[13], args[16])
        results = [shape(c) for c in (DL, DL, QL, QL, DL, DL, KL, KL)]
        return tuple(pl.pallas_call(
            hand_out,
            out_shape=results,
            in_specs=[hbm] * 6,
            out_specs=[hbm] * 8,
            scratch_shapes=[pltpu.VMEM(a.shape, a.dtype) for a in taken + tuple(results)]
            + [sem((6,)), sem((8,))],
            compiler_params=pltpu.CompilerParams(vmem_limit_bytes=63 * 1024 * 1024),
        )(*taken))

    wide = P("seq", "tp")
    flat = P(None, "tp")
    return jax.shard_map(
        step,
        mesh=mesh,
        in_specs=(wide,) * 5 + (flat,) * 12,
        out_specs=(flat,) * 8,
        check_vma=False,
    )
```

```python
import functools
import math

import jax
import jax.numpy as jnp
from jax import lax
from jax.experimental import pallas as pl
from jax.experimental.pallas import tpu as pltpu
from jax.sharding import PartitionSpec as P

HEAD = 128
RANK = 16
GROUP = 4
F32 = jnp.float32
BF16 = jnp.bfloat16
NEG = -1e30


def nt(a, b):
    return lax.dot_general(a, b, (((1,), (1,)), ((), ())), preferred_element_type=F32)


def tn(a, b):
    return lax.dot_general(a, b, (((0,), (0,)), ((), ())), preferred_element_type=F32)


def nn(a, b):
    return jnp.dot(a, b, preferred_element_type=F32)


def kernel(
    n, m, up_per, down_per, keep, X, *refs,
):
    sources = refs[:17]
    held = refs[19:36]
    loaded = refs[-1]
    hidden, qbase, kc, vb, og, qdm, qds, qdn, qum, qus, qun, vdm, vds, vdn, vum, vus, vun = held
    kc, vb = sources[2:4]
    up_out, down_out = refs[17:19]
    (
    kall, vall, vval, vlow_all, lowx, gx, qs, dos, top, tot, wei, dqt, vgs, vgx, vug, quw, up_pack, up_rsx, up_agx, down_pack, down_rsx, down_agx, s_kept, dp_kept,
    k_s, k_r, v_s, v_r, l_s, l_r, x_s, x_r, y_s, y_r, g_s, g_r, ur_s, ur_r, ua_s, ua_r, dr_s, dr_r, da_s, da_r,
    ) = refs[36:-1]
    T, DL = hidden.shape
    KV = kc.shape[1] // HEAD
    rows = GROUP * T
    scale = HEAD ** -0.5
    c2 = scale * math.log2(math.e)
    me = lax.axis_index("seq")
    t = lax.axis_index("tp")

    def to_seq(src, dst, ss, rs, who):
        return pltpu.make_async_remote_copy(
            src_ref=src, dst_ref=dst, send_sem=ss, recv_sem=rs,
            device_id=(who, t), device_id_type=pl.DeviceIdType.MESH,
        )

    def to_tp(src, dst, ss, rs, who):
        return pltpu.make_async_remote_copy(
            src_ref=src, dst_ref=dst, send_sem=ss, recv_sem=rs,
            device_id=(me, who), device_id_type=pl.DeviceIdType.MESH,
        )

    def loop(lo, hi, body):
        def step(i, c):
            body(i)
            return c
        lax.fori_loop(lo, hi, step, 0)

    def load(i):
        dst = held[i]
        if i == 2:
            dst = kall.at[me]
        if i == 3:
            dst = vall.at[me]
        return pltpu.make_async_copy(sources[i], dst, loaded.at[i])

    order = (0, 5, 6, 7, 11, 12, 13, 4, 1, 8, 9, 10, 14, 15, 16, 2, 3)
    for i in order:
        load(i).start()

    barrier = pltpu.get_barrier_semaphore()

    def greet_seq(d):
        pl.semaphore_signal(
            barrier, inc=1, device_id=(lax.rem(me + d, n), t),
            device_id_type=pl.DeviceIdType.MESH,
        )

    def greet_tp(d):
        pl.semaphore_signal(
            barrier, inc=1, device_id=(me, lax.rem(t + d, m)),
            device_id_type=pl.DeviceIdType.MESH,
        )

    loop(1, n, greet_seq)
    loop(1, m, greet_tp)
    pl.semaphore_wait(barrier, n + m - 2)

    x = lax.rem(me, X)
    plane = me - x

    def kv(part, j, who, slot, own=False):
        if part == 0:
            return to_seq(kc if own else kall.at[j], kall.at[j], k_s.at[j, slot], k_r.at[j], who)
        return to_seq(vb if own else vall.at[j], vall.at[j], v_s.at[j, slot], v_r.at[j], who)

    def hand_on(j, part, own, act):
        @pl.when(me + X < n)
        def _():
            act(kv(part, j, me + X, 0, own))

        def across(d):
            other = lax.rem(x + d, X)

            @pl.when(plane + other > j)
            def _():
                act(kv(part, j, plane + other, 1 + other, own))

        loop(1, X, across)

    hand_on(me, 0, True, lambda c: c.start())

    for i in order[:7]:
        load(i).wait()
    qdown = (qdm[...] + qds[...] * qdn[...]).astype(BF16)
    vdown = (vdm[...] + vds[...] * vdn[...]).astype(BF16)
    lowx[t] = jnp.concatenate([nt(qdown, hidden[...]), nt(vdown, hidden[...])], axis=0)

    def x_copy(who):
        return to_tp(lowx.at[t], lowx.at[t], x_s.at[who], x_r.at[t], who)

    def x_in(who):
        return to_tp(lowx.at[who], lowx.at[who], x_s.at[who], x_r.at[who], who)

    loop(1, m, lambda d: x_copy(lax.rem(t + d, m)).start())
    for i in order[7:]:
        load(i).wait()
    qup = (qum[...] + qus[...] * qun[...]).astype(BF16)
    vup = (vum[...] + vus[...] * vun[...]).astype(BF16)
    for g in range(KV):
        for h in range(GROUP):
            at = (g * GROUP + h) * HEAD
            dos[g, h * T:(h + 1) * T, :] = og[:, at:at + HEAD]

    def key_on(j):
        kv(0, j, me, 0).wait_recv()
        hand_on(j, 0, False, lambda c: c.start())

    @pl.when(me >= X)
    def _():
        key_on(me - X)

    loop(1, m, lambda d: x_in(lax.rem(t + d, m)).wait_recv())
    low = lowx[0]
    for i in range(1, m):
        low = low + lowx[i]
    low = low.astype(BF16)
    qlow = low[:RANK]
    vlow = low[RANK:]
    vlow_all[me] = vlow

    def l_copy(who):
        return to_seq(vlow_all.at[me], vlow_all.at[me], l_s.at[who], l_r.at[me], who)

    loop(me + 1, n, lambda who: l_copy(who).start())

    for g in range(KV):
        for h in range(GROUP):
            at = (g * GROUP + h) * HEAD
            q = qbase[:, at:at + HEAD].astype(F32) + tn(qlow, qup[:, at:at + HEAD])
            qs[g, h * T:(h + 1) * T, :] = q.astype(BF16)

    key_pos = lax.broadcasted_iota(jnp.int32, (T, rows), 0)
    row_pos = lax.broadcasted_iota(jnp.int32, (T, rows), 1) % T
    seen = key_pos <= row_pos

    def make_value(j):
        vval[j] = (vall[j].astype(F32) + tn(vlow_all[j], vup)).astype(BF16)

    def scores(j, g, own):
        s = nt(kall[j, :, g * HEAD:(g + 1) * HEAD], qs[g]) * c2
        return jnp.where(seen, s, NEG) if own else s

    def stats(j, own):
        for g in range(KV):
            s = scores(j, g, own)
            if keep:
                s_kept[j, g] = s
            new = jnp.max(s, axis=0, keepdims=True)
            if own:
                tot[g] = jnp.sum(jnp.exp2(s - new), axis=0, keepdims=True)
            else:
                old = top[g]
                new = jnp.maximum(old, new)
                tot[g] = tot[g] * jnp.exp2(old - new) + jnp.sum(
                    jnp.exp2(s - new), axis=0, keepdims=True
                )
            top[g] = new

    stats(me, True)

    def key_column(i):
        j = me - i * X

        @pl.when(i > 1)
        def _():
            key_on(j)

        stats(j, False)

    def across(part, act):
        def visit(j):
            @pl.when(lax.rem(j, X) != x)
            def _():
                kv(part, j, me, 0).wait_recv()
                act(j, False)

        loop(plane, me, visit)
        loop(1, plane + 1, lambda i: visit(plane - i))

    loop(1, me // X + 1, key_column)
    hand_on(me, 1, True, lambda c: c.start())
    across(0, stats)

    for g in range(KV):
        top[g] = top[g] + jnp.log2(tot[g])
    dqt[...] = jnp.zeros_like(dqt)
    vug[...] = jnp.zeros_like(vug)
    wei[...] = jnp.zeros_like(wei)

    def g_copy(j):
        return to_seq(vgs.at[j], vgx.at[me], g_s.at[j], g_r.at[me], j)

    def weigh(j, own):
        make_value(j)
        part = jnp.zeros((RANK, T), F32)
        for g in range(KV):
            cols = slice(g * HEAD, (g + 1) * HEAD)
            p = jnp.exp2((s_kept[j, g] if keep else scores(j, g, own)) - top[g])
            dp = nt(vval[j, :, cols], dos[g])
            if keep:
                s_kept[j, g] = p
                dp_kept[j, g] = dp
            wei[g] += jnp.sum(p * dp, axis=0, keepdims=True)
            dv = nn(p.astype(BF16), dos[g]).astype(BF16)
            part = part + nt(vup[:, cols], dv)
            vug[g] += nn(vlow_all[j], dv)
        vgs[j] = part

    def weigh_other(j, own):
        to_seq(vlow_all.at[j], vlow_all.at[j], l_s.at[j], l_r.at[j], j).wait_recv()
        weigh(j, own)
        g_copy(j).start()

    weigh(me, True)

    def value_column(i):
        j = me - i * X
        kv(1, j, me, 0).wait_recv()
        hand_on(j, 1, False, lambda c: c.start())
        weigh_other(j, False)

    loop(1, me // X + 1, value_column)
    across(1, weigh_other)

    def turn(j, own):
        for g in range(KV):
            cols = slice(g * HEAD, (g + 1) * HEAD)
            if keep:
                p = s_kept[j, g]
                dp = dp_kept[j, g]
            else:
                p = jnp.exp2(scores(j, g, own) - top[g])
                dp = nt(vval[j, :, cols], dos[g])
            ds = (p * (dp - wei[g])).astype(BF16)
            dqt[g] += tn(kall[j, :, cols], ds)

    loop(0, me, lambda j: turn(j, False))
    turn(me, True)

    qg = jnp.zeros((RANK, T), F32)
    for g in range(KV):
        for h in range(GROUP):
            at = (g * GROUP + h) * HEAD
            dq = (dqt[g, :, h * T:(h + 1) * T] * scale).astype(BF16)
            qg = qg + nn(qup[:, at:at + HEAD], dq)
            quw[:, at:at + HEAD] = nt(qlow, dq)

    def deal(tiles, per, pack):
        for i in range(n * per):
            pack[i // per, i % per] = (
                tiles[i].astype(BF16) if i < len(tiles) else jnp.zeros((RANK, HEAD), BF16)
            )

    def others(act):
        loop(1, n, lambda d: act(lax.rem(me + d, n)))

    def r_copy(pack, rsx, ss, rs, who):
        return to_seq(pack.at[who], rsx.at[me], ss.at[who], rs.at[me], who)

    def a_copy(agx, ss, rs, who):
        return to_seq(agx.at[me], agx.at[me], ss.at[who], rs.at[me], who)

    def reduce_in(pack, rsx, agx, ss, rs):
        rsx[me] = pack[me]
        others(lambda w: to_seq(pack.at[w], rsx.at[w], ss.at[w], rs.at[w], w).wait_recv())
        total = rsx[0].astype(F32)
        for i in range(1, n):
            total = total + rsx[i].astype(F32)
        agx[me] = total.astype(BF16)

    def gather_in(agx, ss, rs):
        others(lambda w: to_seq(agx.at[w], agx.at[w], ss.at[w], rs.at[w], w).wait_recv())

    deal(
        [quw[:, k * HEAD:(k + 1) * HEAD] for k in range(KV * GROUP)] + [vug[k] for k in range(KV)],
        up_per, up_pack,
    )
    others(lambda w: r_copy(up_pack, up_rsx, ur_s, ur_r, w).start())

    def g_in(src):
        to_seq(vgs.at[src], vgx.at[src], g_s.at[src], g_r.at[src], src).wait_recv()

    loop(me + 1, n, g_in)
    vg = lax.fori_loop(me + 1, n, lambda s, acc: acc + vgx[s], vgs[me])
    gx[t] = jnp.concatenate([qg, vg], axis=0)

    def y_copy(who):
        return to_tp(gx.at[t], gx.at[t], y_s.at[who], y_r.at[t], who)

    def y_in(who):
        return to_tp(gx.at[who], gx.at[who], y_s.at[who], y_r.at[who], who)

    loop(1, m, lambda d: y_copy(lax.rem(t + d, m)).start())
    loop(1, m, lambda d: y_in(lax.rem(t + d, m)).wait_recv())
    lg = gx[0]
    for i in range(1, m):
        lg = lg + gx[i]
    dg = nn(lg.astype(BF16), hidden[...])

    deal(
        [dg[:RANK, k * HEAD:(k + 1) * HEAD] for k in range(DL // HEAD)]
        + [dg[RANK:, k * HEAD:(k + 1) * HEAD] for k in range(DL // HEAD)],
        down_per, down_pack,
    )
    others(lambda w: r_copy(down_pack, down_rsx, dr_s, dr_r, w).start())
    reduce_in(up_pack, up_rsx, up_agx, ur_s, ur_r)
    others(lambda w: a_copy(up_agx, ua_s, ua_r, w).start())
    reduce_in(down_pack, down_rsx, down_agx, dr_s, dr_r)
    others(lambda w: a_copy(down_agx, da_s, da_r, w).start())
    gather_in(up_agx, ua_s, ua_r)
    up_out[...] = up_agx[...]
    gather_in(down_agx, da_s, da_r)
    down_out[...] = down_agx[...]

    def drain_later(who):
        l_copy(who).wait_send()

    loop(me + 1, n, drain_later)
    loop(0, me, lambda j: g_copy(j).wait_send())
    for part in range(2):
        hand_on(me, part, True, lambda c: c.wait_send())
        loop(1, me // X + 1, lambda i: hand_on(me - i * X, part, False, lambda c: c.wait_send()))

    def drain_tp(d):
        who = lax.rem(t + d, m)
        x_copy(who).wait_send()
        y_copy(who).wait_send()

    loop(1, m, drain_tp)

    def drain_seq(d):
        who = lax.rem(me + d, n)
        r_copy(up_pack, up_rsx, ur_s, ur_r, who).wait_send()
        a_copy(up_agx, ua_s, ua_r, who).wait_send()
        r_copy(down_pack, down_rsx, dr_s, dr_r, who).wait_send()
        a_copy(down_agx, da_s, da_r, who).wait_send()

    loop(1, n, drain_seq)


def hand_out(*refs):
    up, down = refs[6 + 8:6 + 8 + 2]
    noises = refs[16:20]
    outs = refs[20:28]
    in_sem, out_sem = refs[28:]
    loads = [
        pltpu.make_async_copy(refs[i], refs[14 + i], in_sem.at[i]) for i in range(6)
    ]
    stores = [
        pltpu.make_async_copy(outs[i], refs[6 + i], out_sem.at[i]) for i in range(8)
    ]
    for c in loads:
        c.start()
    for c in loads:
        c.wait()
    per = (up.shape[1], down.shape[1])
    at = [0, 0]
    for which, i in ((1, 0), (1, 2), (0, 1), (0, 3)):
        for k in range(noises[i].shape[1] // HEAD):
            unit = at[which]
            at[which] += 1
            cols = slice(k * HEAD, (k + 1) * HEAD)
            value = (up, down)[which][unit // per[which], unit % per[which]].astype(F32)
            outs[2 * i][:, cols] = value
            outs[2 * i + 1][:, cols] = value * noises[i][:, cols]
        stores[2 * i].start()
        stores[2 * i + 1].start()
    for c in stores:
        c.wait()


def solution(mesh):
    n = mesh.shape["seq"]
    m = mesh.shape["tp"]

    def step(*args):
        hidden, qbase, kc = args[:3]
        T, DL = hidden.shape
        QL, KL = qbase.shape[1], kc.shape[1]
        KV = KL // HEAD
        rows = GROUP * T
        up_per = -(-(QL + KL) // (HEAD * n))
        down_per = -(-2 * DL // (HEAD * n))
        keep = n * KV * T * rows * 8 <= 36 * 1024 * 1024
        kept = (n, KV, T, rows) if keep else (1, 1, 8, HEAD)
        shape = lambda cols: jax.ShapeDtypeStruct((RANK, cols), F32)
        X = 1
        while 2 * (2 * X) ** 2 <= n:
            X *= 2
        hbm = pl.BlockSpec(memory_space=pltpu.HBM)
        vmem = pl.BlockSpec(memory_space=pltpu.VMEM)
        sem = pltpu.SemaphoreType.DMA
        outs = pl.pallas_call(
            functools.partial(kernel, n, m, up_per, down_per, keep, X),
            out_shape=[
                jax.ShapeDtypeStruct((n, up_per, RANK, HEAD), BF16),
                jax.ShapeDtypeStruct((n, down_per, RANK, HEAD), BF16),
            ],
            in_specs=[hbm] * 17,
            out_specs=[vmem] * 2,
            scratch_shapes=[pltpu.VMEM(a.shape, a.dtype) for a in args] + [
                pltpu.VMEM((n, T, KL), BF16),
                pltpu.VMEM((n, T, KL), BF16),
                pltpu.VMEM((n, T, KL), BF16),
                pltpu.VMEM((n, RANK, T), BF16),
                pltpu.VMEM((m, 2 * RANK, T), F32),
                pltpu.VMEM((m, 2 * RANK, T), F32),
                pltpu.VMEM((KV, rows, HEAD), BF16),
                pltpu.VMEM((KV, rows, HEAD), BF16),
                pltpu.VMEM((KV, 1, rows), F32),
                pltpu.VMEM((KV, 1, rows), F32),
                pltpu.VMEM((KV, 1, rows), F32),
                pltpu.VMEM((KV, HEAD, rows), F32),
                pltpu.VMEM((n, RANK, T), F32),
                pltpu.VMEM((n, RANK, T), F32),
                pltpu.VMEM((KV, RANK, HEAD), F32),
                pltpu.VMEM((RANK, QL), F32),
            ] + [pltpu.VMEM((n, up_per, RANK, HEAD), BF16)] * 3
            + [pltpu.VMEM((n, down_per, RANK, HEAD), BF16)] * 3 + [
                pltpu.VMEM(kept, F32),
                pltpu.VMEM(kept, F32),
            ] + [sem((n, 1 + X)), sem((n,)), sem((n, 1 + X)), sem((n,))]
            + [sem((k,)) for k in (n, n, m, m, m, m) + (n,) * 10 + (17,)],
            compiler_params=pltpu.CompilerParams(
                collective_id=0, has_side_effects=True, vmem_limit_bytes=63 * 1024 * 1024
            ),
            cost_estimate=pl.CostEstimate(
                flops=14 * rows * KV * n * T * HEAD // 2,
                bytes_accessed=8 * 1024 * 1024,
                transcendentals=rows * KV * n * T,
            ),
        )(*args)
        taken = tuple(outs) + (args[7], args[10], args[13], args[16])
        results = [shape(c) for c in (DL, DL, QL, QL, DL, DL, KL, KL)]
        return tuple(pl.pallas_call(
            hand_out,
            out_shape=results,
            in_specs=[hbm] * 6,
            out_specs=[hbm] * 8,
            scratch_shapes=[pltpu.VMEM(a.shape, a.dtype) for a in taken + tuple(results)]
            + [sem((6,)), sem((8,))],
            compiler_params=pltpu.CompilerParams(vmem_limit_bytes=63 * 1024 * 1024),
        )(*taken))

    wide = P("seq", "tp")
    flat = P(None, "tp")
    return jax.shard_map(
        step,
        mesh=mesh,
        in_specs=(wide,) * 5 + (flat,) * 12,
        out_specs=(flat,) * 8,
        check_vma=False,
    )
```

```python
import functools
import math

import jax
import jax.numpy as jnp
from jax import lax
from jax.experimental import pallas as pl
from jax.experimental.pallas import tpu as pltpu
from jax.sharding import PartitionSpec as P

HEAD = 128
RANK = 16
GROUP = 4
F32 = jnp.float32
BF16 = jnp.bfloat16
NEG = -1e30


def nt(a, b):
    return lax.dot_general(a, b, (((1,), (1,)), ((), ())), preferred_element_type=F32)


def tn(a, b):
    return lax.dot_general(a, b, (((0,), (0,)), ((), ())), preferred_element_type=F32)


def nn(a, b):
    return jnp.dot(a, b, preferred_element_type=F32)


def kernel(
    n, m, up_per, down_per, keep, X, *refs,
):
    sources = refs[:17]
    held = refs[19:36]
    loaded = refs[-1]
    hidden, qbase, kc, vb, og, qdm, qds, qdn, qum, qus, qun, vdm, vds, vdn, vum, vus, vun = held
    kc, vb = sources[2:4]
    up_out, down_out = refs[17:19]
    (
    kall, vall, vval, vlow_all, lowx, gx, qs, dos, top, tot, wei, dqt, vgs, vgx, vug, quw, up_pack, up_rsx, up_agx, down_pack, down_rsx, down_agx, s_kept, dp_kept,
    k_s, k_r, v_s, v_r, l_s, l_r, x_s, x_r, y_s, y_r, g_s, g_r, ur_s, ur_r, ua_s, ua_r, dr_s, dr_r, da_s, da_r,
    ) = refs[36:-1]
    T, DL = hidden.shape
    KV = kc.shape[1] // HEAD
    rows = GROUP * T
    scale = HEAD ** -0.5
    c2 = scale * math.log2(math.e)
    me = lax.axis_index("seq")
    t = lax.axis_index("tp")

    def to_seq(src, dst, ss, rs, who):
        return pltpu.make_async_remote_copy(
            src_ref=src, dst_ref=dst, send_sem=ss, recv_sem=rs,
            device_id=(who, t), device_id_type=pl.DeviceIdType.MESH,
        )

    def to_tp(src, dst, ss, rs, who):
        return pltpu.make_async_remote_copy(
            src_ref=src, dst_ref=dst, send_sem=ss, recv_sem=rs,
            device_id=(me, who), device_id_type=pl.DeviceIdType.MESH,
        )

    def loop(lo, hi, body):
        def step(i, c):
            body(i)
            return c
        lax.fori_loop(lo, hi, step, 0)

    def load(i):
        dst = held[i]
        if i == 2:
            dst = kall.at[me]
        if i == 3:
            dst = vall.at[me]
        return pltpu.make_async_copy(sources[i], dst, loaded.at[i])

    order = (0, 5, 6, 7, 11, 12, 13, 4, 1, 8, 9, 10, 14, 15, 16, 2, 3)
    for i in order:
        load(i).start()

    barrier = pltpu.get_barrier_semaphore()

    def greet_seq(d):
        pl.semaphore_signal(
            barrier, inc=1, device_id=(lax.rem(me + d, n), t),
            device_id_type=pl.DeviceIdType.MESH,
        )

    def greet_tp(d):
        pl.semaphore_signal(
            barrier, inc=1, device_id=(me, lax.rem(t + d, m)),
            device_id_type=pl.DeviceIdType.MESH,
        )

    loop(1, n, greet_seq)
    loop(1, m, greet_tp)
    pl.semaphore_wait(barrier, n + m - 2)

    x = lax.rem(me, X)
    plane = me - x

    def kv(part, j, who, slot, own=False):
        if part == 0:
            return to_seq(kc if own else kall.at[j], kall.at[j], k_s.at[j, slot], k_r.at[j], who)
        return to_seq(vb if own else vall.at[j], vall.at[j], v_s.at[j, slot], v_r.at[j], who)

    def hand_on(j, part, own, act):
        @pl.when(me + X < n)
        def _():
            act(kv(part, j, me + X, 0, own))

        def across(d):
            other = lax.rem(x + d, X)

            @pl.when(plane + other > j)
            def _():
                act(kv(part, j, plane + other, 1 + other, own))

        loop(1, X, across)

    hand_on(me, 0, True, lambda c: c.start())

    for i in order[:7]:
        load(i).wait()
    qdown = (qdm[...] + qds[...] * qdn[...]).astype(BF16)
    vdown = (vdm[...] + vds[...] * vdn[...]).astype(BF16)
    lowx[t] = jnp.concatenate([nt(qdown, hidden[...]), nt(vdown, hidden[...])], axis=0)

    def x_copy(who):
        return to_tp(lowx.at[t], lowx.at[t], x_s.at[who], x_r.at[t], who)

    def x_in(who):
        return to_tp(lowx.at[who], lowx.at[who], x_s.at[who], x_r.at[who], who)

    loop(1, m, lambda d: x_copy(lax.rem(t + d, m)).start())
    for i in order[7:]:
        load(i).wait()
    qup = (qum[...] + qus[...] * qun[...]).astype(BF16)
    vup = (vum[...] + vus[...] * vun[...]).astype(BF16)
    for g in range(KV):
        for h in range(GROUP):
            at = (g * GROUP + h) * HEAD
            dos[g, h * T:(h + 1) * T, :] = og[:, at:at + HEAD]

    def key_on(j):
        kv(0, j, me, 0).wait_recv()
        hand_on(j, 0, False, lambda c: c.start())

    @pl.when(me >= X)
    def _():
        key_on(me - X)

    loop(1, m, lambda d: x_in(lax.rem(t + d, m)).wait_recv())
    low = lowx[0]
    for i in range(1, m):
        low = low + lowx[i]
    low = low.astype(BF16)
    qlow = low[:RANK]
    vlow = low[RANK:]
    vlow_all[me] = vlow

    def l_copy(who):
        return to_seq(vlow_all.at[me], vlow_all.at[me], l_s.at[who], l_r.at[me], who)

    loop(me + 1, n, lambda who: l_copy(who).start())

    for g in range(KV):
        for h in range(GROUP):
            at = (g * GROUP + h) * HEAD
            q = qbase[:, at:at + HEAD].astype(F32) + tn(qlow, qup[:, at:at + HEAD])
            qs[g, h * T:(h + 1) * T, :] = q.astype(BF16)

    key_pos = lax.broadcasted_iota(jnp.int32, (T, T), 0)
    row_pos = lax.broadcasted_iota(jnp.int32, (T, T), 1)
    seen = key_pos <= row_pos

    def make_value(j):
        vval[j] = (vall[j].astype(F32) + tn(vlow_all[j], vup)).astype(BF16)

    heads = [slice(h * T, (h + 1) * T) for h in range(GROUP)]

    def scores(j, g, r, own):
        s = nt(kall[j, :, g * HEAD:(g + 1) * HEAD], qs[g, r, :]) * c2
        return jnp.where(seen, s, NEG) if own else s

    def stats(j, own):
        for g, r in [(g, r) for g in range(KV) for r in heads]:
            s = scores(j, g, r, own)
            if keep:
                s_kept[j, g, :, r] = s
            new = jnp.max(s, axis=0, keepdims=True)
            if own:
                tot[g, :, r] = jnp.sum(jnp.exp2(s - new), axis=0, keepdims=True)
            else:
                old = top[g, :, r]
                new = jnp.maximum(old, new)
                tot[g, :, r] = tot[g, :, r] * jnp.exp2(old - new) + jnp.sum(
                    jnp.exp2(s - new), axis=0, keepdims=True
                )
            top[g, :, r] = new

    stats(me, True)

    def key_column(i):
        j = me - i * X

        @pl.when(i > 1)
        def _():
            key_on(j)

        stats(j, False)

    def across(part, act):
        def visit(j):
            @pl.when(lax.rem(j, X) != x)
            def _():
                kv(part, j, me, 0).wait_recv()
                act(j, False)

        loop(plane, me, visit)
        loop(1, plane + 1, lambda i: visit(plane - i))

    loop(1, me // X + 1, key_column)
    hand_on(me, 1, True, lambda c: c.start())
    across(0, stats)

    for g in range(KV):
        top[g] = top[g] + jnp.log2(tot[g])
    dqt[...] = jnp.zeros_like(dqt)
    vug[...] = jnp.zeros_like(vug)
    wei[...] = jnp.zeros_like(wei)

    def g_copy(j):
        return to_seq(vgs.at[j], vgx.at[me], g_s.at[j], g_r.at[me], j)

    def weigh(j, own):
        make_value(j)
        part = jnp.zeros((RANK, T), F32)
        for g in range(KV):
            cols = slice(g * HEAD, (g + 1) * HEAD)
            dv = jnp.zeros((T, HEAD), F32)
            for r in heads:
                p = jnp.exp2((s_kept[j, g, :, r] if keep else scores(j, g, r, own)) - top[g, :, r])
                dp = nt(vval[j, :, cols], dos[g, r, :])
                if keep:
                    s_kept[j, g, :, r] = p
                    dp_kept[j, g, :, r] = dp
                wei[g, :, r] += jnp.sum(p * dp, axis=0, keepdims=True)
                dv = dv + nn(p.astype(BF16), dos[g, r, :])
            dv = dv.astype(BF16)
            part = part + nt(vup[:, cols], dv)
            vug[g] += nn(vlow_all[j], dv)
        vgs[j] = part

    def weigh_other(j, own):
        to_seq(vlow_all.at[j], vlow_all.at[j], l_s.at[j], l_r.at[j], j).wait_recv()
        weigh(j, own)
        g_copy(j).start()

    weigh(me, True)

    def value_column(i):
        j = me - i * X
        kv(1, j, me, 0).wait_recv()
        hand_on(j, 1, False, lambda c: c.start())
        weigh_other(j, False)

    loop(1, me // X + 1, value_column)
    across(1, weigh_other)

    def turn(j, own):
        for g in range(KV):
            cols = slice(g * HEAD, (g + 1) * HEAD)
            for r in heads:
                if keep:
                    p = s_kept[j, g, :, r]
                    dp = dp_kept[j, g, :, r]
                else:
                    p = jnp.exp2(scores(j, g, r, own) - top[g, :, r])
                    dp = nt(vval[j, :, cols], dos[g, r, :])
                ds = (p * (dp - wei[g, :, r])).astype(BF16)
                dqt[g, :, r] += tn(kall[j, :, cols], ds)

    loop(0, me, lambda j: turn(j, False))
    turn(me, True)

    qg = jnp.zeros((RANK, T), F32)
    for g in range(KV):
        for h in range(GROUP):
            at = (g * GROUP + h) * HEAD
            dq = (dqt[g, :, h * T:(h + 1) * T] * scale).astype(BF16)
            qg = qg + nn(qup[:, at:at + HEAD], dq)
            quw[:, at:at + HEAD] = nt(qlow, dq)

    def deal(tiles, per, pack):
        for i in range(n * per):
            pack[i // per, i % per] = (
                tiles[i].astype(BF16) if i < len(tiles) else jnp.zeros((RANK, HEAD), BF16)
            )

    def others(act):
        loop(1, n, lambda d: act(lax.rem(me + d, n)))

    def r_copy(pack, rsx, ss, rs, who):
        return to_seq(pack.at[who], rsx.at[me], ss.at[who], rs.at[me], who)

    def a_copy(agx, ss, rs, who):
        return to_seq(agx.at[me], agx.at[me], ss.at[who], rs.at[me], who)

    def reduce_in(pack, rsx, agx, ss, rs):
        rsx[me] = pack[me]
        others(lambda w: to_seq(pack.at[w], rsx.at[w], ss.at[w], rs.at[w], w).wait_recv())
        total = rsx[0].astype(F32)
        for i in range(1, n):
            total = total + rsx[i].astype(F32)
        agx[me] = total.astype(BF16)

    def gather_in(agx, ss, rs):
        others(lambda w: to_seq(agx.at[w], agx.at[w], ss.at[w], rs.at[w], w).wait_recv())

    deal(
        [quw[:, k * HEAD:(k + 1) * HEAD] for k in range(KV * GROUP)] + [vug[k] for k in range(KV)],
        up_per, up_pack,
    )
    others(lambda w: r_copy(up_pack, up_rsx, ur_s, ur_r, w).start())

    def g_in(src):
        to_seq(vgs.at[src], vgx.at[src], g_s.at[src], g_r.at[src], src).wait_recv()

    loop(me + 1, n, g_in)
    vg = lax.fori_loop(me + 1, n, lambda s, acc: acc + vgx[s], vgs[me])
    gx[t] = jnp.concatenate([qg, vg], axis=0)

    def y_copy(who):
        return to_tp(gx.at[t], gx.at[t], y_s.at[who], y_r.at[t], who)

    def y_in(who):
        return to_tp(gx.at[who], gx.at[who], y_s.at[who], y_r.at[who], who)

    loop(1, m, lambda d: y_copy(lax.rem(t + d, m)).start())
    loop(1, m, lambda d: y_in(lax.rem(t + d, m)).wait_recv())
    lg = gx[0]
    for i in range(1, m):
        lg = lg + gx[i]
    dg = nn(lg.astype(BF16), hidden[...])

    deal(
        [dg[:RANK, k * HEAD:(k + 1) * HEAD] for k in range(DL // HEAD)]
        + [dg[RANK:, k * HEAD:(k + 1) * HEAD] for k in range(DL // HEAD)],
        down_per, down_pack,
    )
    others(lambda w: r_copy(down_pack, down_rsx, dr_s, dr_r, w).start())
    reduce_in(up_pack, up_rsx, up_agx, ur_s, ur_r)
    others(lambda w: a_copy(up_agx, ua_s, ua_r, w).start())
    reduce_in(down_pack, down_rsx, down_agx, dr_s, dr_r)
    others(lambda w: a_copy(down_agx, da_s, da_r, w).start())
    gather_in(up_agx, ua_s, ua_r)
    up_out[...] = up_agx[...]
    gather_in(down_agx, da_s, da_r)
    down_out[...] = down_agx[...]

    def drain_later(who):
        l_copy(who).wait_send()

    loop(me + 1, n, drain_later)
    loop(0, me, lambda j: g_copy(j).wait_send())
    for part in range(2):
        hand_on(me, part, True, lambda c: c.wait_send())
        loop(1, me // X + 1, lambda i: hand_on(me - i * X, part, False, lambda c: c.wait_send()))

    def drain_tp(d):
        who = lax.rem(t + d, m)
        x_copy(who).wait_send()
        y_copy(who).wait_send()

    loop(1, m, drain_tp)

    def drain_seq(d):
        who = lax.rem(me + d, n)
        r_copy(up_pack, up_rsx, ur_s, ur_r, who).wait_send()
        a_copy(up_agx, ua_s, ua_r, who).wait_send()
        r_copy(down_pack, down_rsx, dr_s, dr_r, who).wait_send()
        a_copy(down_agx, da_s, da_r, who).wait_send()

    loop(1, n, drain_seq)


def hand_out(*refs):
    up, down = refs[6 + 8:6 + 8 + 2]
    noises = refs[16:20]
    outs = refs[20:28]
    in_sem, out_sem = refs[28:]
    loads = [
        pltpu.make_async_copy(refs[i], refs[14 + i], in_sem.at[i]) for i in range(6)
    ]
    stores = [
        pltpu.make_async_copy(outs[i], refs[6 + i], out_sem.at[i]) for i in range(8)
    ]
    for c in loads:
        c.start()
    for c in loads:
        c.wait()
    per = (up.shape[1], down.shape[1])
    at = [0, 0]
    for which, i in ((1, 0), (1, 2), (0, 1), (0, 3)):
        for k in range(noises[i].shape[1] // HEAD):
            unit = at[which]
            at[which] += 1
            cols = slice(k * HEAD, (k + 1) * HEAD)
            value = (up, down)[which][unit // per[which], unit % per[which]].astype(F32)
            outs[2 * i][:, cols] = value
            outs[2 * i + 1][:, cols] = value * noises[i][:, cols]
        stores[2 * i].start()
        stores[2 * i + 1].start()
    for c in stores:
        c.wait()


def solution(mesh):
    n = mesh.shape["seq"]
    m = mesh.shape["tp"]

    def step(*args):
        hidden, qbase, kc = args[:3]
        T, DL = hidden.shape
        QL, KL = qbase.shape[1], kc.shape[1]
        KV = KL // HEAD
        rows = GROUP * T
        up_per = -(-(QL + KL) // (HEAD * n))
        down_per = -(-2 * DL // (HEAD * n))
        keep = n * KV * T * rows * 8 <= 36 * 1024 * 1024
        kept = (n, KV, T, rows) if keep else (1, 1, 8, HEAD)
        shape = lambda cols: jax.ShapeDtypeStruct((RANK, cols), F32)
        X = 1
        while 2 * (2 * X) ** 2 <= n:
            X *= 2
        hbm = pl.BlockSpec(memory_space=pltpu.HBM)
        vmem = pl.BlockSpec(memory_space=pltpu.VMEM)
        sem = pltpu.SemaphoreType.DMA
        outs = pl.pallas_call(
            functools.partial(kernel, n, m, up_per, down_per, keep, X),
            out_shape=[
                jax.ShapeDtypeStruct((n, up_per, RANK, HEAD), BF16),
                jax.ShapeDtypeStruct((n, down_per, RANK, HEAD), BF16),
            ],
            in_specs=[hbm] * 17,
            out_specs=[vmem] * 2,
            scratch_shapes=[pltpu.VMEM(a.shape, a.dtype) for a in args] + [
                pltpu.VMEM((n, T, KL), BF16),
                pltpu.VMEM((n, T, KL), BF16),
                pltpu.VMEM((n, T, KL), BF16),
                pltpu.VMEM((n, RANK, T), BF16),
                pltpu.VMEM((m, 2 * RANK, T), F32),
                pltpu.VMEM((m, 2 * RANK, T), F32),
                pltpu.VMEM((KV, rows, HEAD), BF16),
                pltpu.VMEM((KV, rows, HEAD), BF16),
                pltpu.VMEM((KV, 1, rows), F32),
                pltpu.VMEM((KV, 1, rows), F32),
                pltpu.VMEM((KV, 1, rows), F32),
                pltpu.VMEM((KV, HEAD, rows), F32),
                pltpu.VMEM((n, RANK, T), F32),
                pltpu.VMEM((n, RANK, T), F32),
                pltpu.VMEM((KV, RANK, HEAD), F32),
                pltpu.VMEM((RANK, QL), F32),
            ] + [pltpu.VMEM((n, up_per, RANK, HEAD), BF16)] * 3
            + [pltpu.VMEM((n, down_per, RANK, HEAD), BF16)] * 3 + [
                pltpu.VMEM(kept, F32),
                pltpu.VMEM(kept, F32),
            ] + [sem((n, 1 + X)), sem((n,)), sem((n, 1 + X)), sem((n,))]
            + [sem((k,)) for k in (n, n, m, m, m, m) + (n,) * 10 + (17,)],
            compiler_params=pltpu.CompilerParams(
                collective_id=0, has_side_effects=True, vmem_limit_bytes=63 * 1024 * 1024
            ),
            cost_estimate=pl.CostEstimate(
                flops=14 * rows * KV * n * T * HEAD // 2,
                bytes_accessed=8 * 1024 * 1024,
                transcendentals=rows * KV * n * T,
            ),
        )(*args)
        taken = tuple(outs) + (args[7], args[10], args[13], args[16])
        results = [shape(c) for c in (DL, DL, QL, QL, DL, DL, KL, KL)]
        return tuple(pl.pallas_call(
            hand_out,
            out_shape=results,
            in_specs=[hbm] * 6,
            out_specs=[hbm] * 8,
            scratch_shapes=[pltpu.VMEM(a.shape, a.dtype) for a in taken + tuple(results)]
            + [sem((6,)), sem((8,))],
            compiler_params=pltpu.CompilerParams(vmem_limit_bytes=63 * 1024 * 1024),
        )(*taken))

    wide = P("seq", "tp")
    flat = P(None, "tp")
    return jax.shard_map(
        step,
        mesh=mesh,
        in_specs=(wide,) * 5 + (flat,) * 12,
        out_specs=(flat,) * 8,
        check_vma=False,
    )
```
